32 devices in a mesh: req: 8 (over y, x, core), exp: 4 (over z).
Axes of the slice: x: 2, y: 2, z: 4, core: 2. Of those that a mesh axis runs over, the one named last changes fastest.
Arguments:
- resid_in: bfloat16 [256, 3584], P(('req', 'exp')), may hold values from -6 to 6
- queries: bfloat16 [256, 3584], P(('req', 'exp')), may hold values from -40 to 40
- fresh_kv: bfloat16 [256, 1024], P(('req', 'exp')), may hold values from -6 to 6
- kv_pool: bfloat16 [8, 4, 32, 16, 1024], P('req', 'exp'), may hold values from -6 to 6
- block_table: int32 [128, 8], P(('req', 'exp')), may hold values from 0 to 31, as said below
- lengths: int32 [128], P(('req', 'exp')), may hold values from 1 to 128, as said below
- mig_source: int32 [8, 4, 2, 4], P('req', 'exp'), may hold values from 0 to 31, as said below
- mig_target: int32 [8, 4, 2, 4], P('req', 'exp'), may hold values from 0 to 31, as said below
- expert_ids: int32 [256, 8], P('req'), may hold values from 0 to 15, all different within a row; in each aligned block of 32 rows (0 to 31, 32 to 63, ...) at most 24 rows name the same one
- gate_values: float32 [256, 8], P('req'), may hold values from 0.2 to 1
- norm_gain: bfloat16 [3584], replicated, may hold values from 0.5 to 1.5
- w_in: bfloat16 [4, 8, 3584, 1024], P('exp', 'req'), may hold values from -0.09375 to 0.09375
- w_out: bfloat16 [4, 8, 1024, 3584], P('exp', 'req'), may hold values from -0.125 to 0.125
Outputs:
- mixed: bfloat16 [256, 3584], P(('req', 'exp'))
The draws below stay inside these ranges and needn't reach their ends.
Inputs may be any that keep to these rules, and one draw needn't show every extreme that they name: `block_table`: the entries of the 4 rows of one device are distinct pages of that device's pool. `lengths`: A request that arrives by migration has more than (3) * 16 cached positions. `mig_target`: on every device exactly one request arrives from req index - 1 and one from index + 1 (around the loop); [r, e, 0, i] is the page that takes page i of the request from index - 1, [r, e, 1, i] of the one from index + 1; they are the first 4 entries of that request's block-table row. `mig_source`: [r, e, 0, i] is the pool page sent as page i to index + 1, [r, e, 1, i] to index - 1; the 8 pages of a device are distinct and belong to no request that stays on it. `expert_ids`: each row names 8 different experts; among the 32 tokens of one index of req no expert is named by more than 24 rows.
All inputs are finite; a program needn't handle non-finite values.
Results may differ from the reference program's by a relative error of at most 0.012.
Values may be sent and summed in bfloat16 or wider, within the bound.
No kernel may reach another device: no remote copies, remote signals or barrier semaphores. Data moves between devices by JAX's collectives and lax.ppermute only.
A program may use at most 64 MiB of HBM per device.

```python
import math
import jax
import jax.numpy as jnp
import numpy as np
from jax import lax

D = 3584
HEADS = 28
KV_HEADS = 4
HEAD_DIM = 128
TOPK = 8
EXPERTS = 16
FF = 2048
GRP = 2
FH = 1024
REQ_DEV = 4
DRAFT = 2
TOK = 8
PAGE = 16
MAXP = 8
MIGP = 4
CTX = 128
KVW = 1024
PAGES_DEV = 32
REQUESTS = 128
TOKENS = 256
CAP = 24
N_REQ = 8
N_EXP = 4


def page_plan(key):
    base = jax.random.fold_in(key, 71)
    device_count = N_REQ * N_EXP
    order_key, slot_key, stay_key, move_key, rank_key = jax.random.split(base, 5)
    page_order = jax.vmap(lambda sub_key: jax.random.permutation(sub_key, PAGES_DEV))(jax.random.split(order_key, device_count))
    slot_order = jax.vmap(lambda sub_key: jax.random.permutation(sub_key, REQ_DEV))(jax.random.split(slot_key, device_count))
    tables = page_order.reshape(device_count, REQ_DEV, MAXP).astype(jnp.int32)
    from_left = slot_order[:, 0]
    from_right = slot_order[:, 1]
    first_stay = slot_order[:, 2]
    slot_ids = jnp.arange(REQ_DEV)[None, :]
    arriving = (slot_ids == from_left[:, None]) | (slot_ids == from_right[:, None])
    stay_lengths = jax.random.randint(stay_key, (device_count, REQ_DEV), 1, CTX + 1)
    move_lengths = jax.random.randint(move_key, (device_count, REQ_DEV), (MIGP - 1) * PAGE + 1, MIGP * PAGE + 1)
    request_lengths = jnp.where(arriving, move_lengths, stay_lengths)
    device_ids = jnp.arange(device_count)[:, None]
    request_lengths = jnp.where((device_ids == 0) & (slot_ids == first_stay[:, None]), CTX, request_lengths)
    request_lengths = jnp.where((device_ids == 0) & (slot_ids == from_left[:, None]), MIGP * PAGE, request_lengths).astype(jnp.int32)
    left_rows = jnp.take_along_axis(tables, from_left[:, None, None], axis=1)[:, 0, :MIGP]
    right_rows = jnp.take_along_axis(tables, from_right[:, None, None], axis=1)[:, 0, :MIGP]
    targets = jnp.stack([left_rows, right_rows], axis=1).astype(jnp.int32)
    page_counts = (request_lengths + PAGE - 1) // PAGE
    entry_used = jnp.logical_not(arriving)[:, :, None] & (jnp.arange(MAXP)[None, None, :] < page_counts[:, :, None])
    staying = jnp.any((tables[:, :, :, None] == jnp.arange(PAGES_DEV)[None, None, None, :]) & entry_used[:, :, :, None], axis=(1, 2))
    ranks = jax.vmap(lambda sub_key: jax.random.permutation(sub_key, PAGES_DEV))(jax.random.split(rank_key, device_count))
    ranks = (ranks + jnp.where(staying, PAGES_DEV, 0)).astype(jnp.int32)
    chosen = lax.top_k(-ranks, 2 * MIGP)[1].astype(jnp.int32)
    sources = jnp.stack([chosen[:, :MIGP], chosen[:, MIGP:]], axis=1)
    return (tables.reshape(REQUESTS, MAXP), request_lengths.reshape(REQUESTS), sources.reshape(N_REQ, N_EXP, 2, MIGP), targets.reshape(N_REQ, N_EXP, 2, MIGP))


def draw_block_table(key, part):
    return page_plan(key)[0]


def draw_lengths(key, part):
    return page_plan(key)[1]


def draw_mig_source(key, part):
    return page_plan(key)[2]


def draw_mig_target(key, part):
    return page_plan(key)[3]


def token_draws(key):
    base = jax.random.fold_in(key, 29)
    query_key, fresh_key = jax.random.split(base, 2)
    query_rows = jnp.clip(jax.random.normal(query_key, (TOKENS, HEADS * HEAD_DIM), jnp.float32), -6.0, 6.0)
    fresh_rows = jnp.clip(jax.random.normal(fresh_key, (TOKENS, KVW), jnp.float32), -6.0, 6.0)
    return (query_rows.astype(jnp.bfloat16), fresh_rows.astype(jnp.bfloat16))


def draw_queries(key, part):
    return token_draws(key)[0]


def draw_fresh_kv(key, part):
    return token_draws(key)[1]


def block_scale(key, shape, shards, smallest, high):
    level = 1.0
    for dim, parts in shards:
        draws = jax.random.uniform(jax.random.fold_in(jax.random.fold_in(key, 6), dim), (parts,), jnp.float32, smallest / len(shards), high / len(shards))
        level = level * jnp.repeat(jnp.exp(draws), shape[dim] // parts).reshape((-1,) + (1,) * (len(shape) - 1 - dim))
    return level


def routed_block(rng, own, number, rows, count, top, bound, skew):
    order = jax.random.permutation(rng, count)
    crowded, usual = portions_of(count, rows * top, bound, skew, True), portions_of(count, rows * top, bound, skew, False)
    places = jnp.arange(count)

    def named(sizes, turn):
        used = int((sizes > 0).sum())
        fixed = max(1, used // 4)
        passed = fixed + (places - fixed + turn * (used - fixed)) % max(1, count - fixed)
        return jnp.zeros((count,), jnp.int32).at[order[jnp.where(places < fixed, places, passed)]].set(jnp.asarray(sizes, jnp.int32))

    sizes = jnp.where(number % 4 == 0, named(crowded, number // 4), named(usual, number - number // 4 - 1))
    mixed = jax.random.permutation(jax.random.fold_in(own, 3), count)
    donor, receiver = mixed[0:count // 2 * 2:2], mixed[1:count // 2 * 2:2]
    margin = jnp.minimum(sizes[donor] - 1, bound - sizes[receiver]) // 2
    margin = jnp.where((donor == order[0]) | (receiver == order[0]) | (sizes[receiver] == 0), 0, jnp.maximum(margin, 0))
    passed = jax.random.randint(jax.random.fold_in(own, 4), (count // 2,), 0, 1 << 20) % (margin + 1)
    sizes = sizes.at[donor].add(-passed).at[receiver].add(passed)
    labels = jnp.searchsorted(jnp.cumsum(sizes), jnp.arange(rows * top), side="right").astype(jnp.int32)
    table = labels.reshape(top, rows).T
    table = table[jax.random.permutation(jax.random.fold_in(own, 1), rows)]
    turn = jax.random.randint(jax.random.fold_in(own, 2), (rows, 1), 0, top)
    return jnp.take_along_axis(table, (jnp.arange(top)[None, :] + turn) % top, axis=1)


def portions_of(number_of, total, reach, slope, full):
    loads = [(1 << 20) // math.isqrt(standing ** slope) + 1 for standing in range(1, number_of + 1)]
    largest = reach if full else min(reach, max(-(-total // number_of), total * loads[0] // sum(loads)))
    least = 1 if total - largest >= number_of - 1 else 0
    holding, spare = [largest] + [least] * (number_of - 1), total - largest - least * (number_of - 1)
    while spare > 0:
        candidates = [i for i in range(1, number_of) if holding[i] < largest] or [i for i in range(1, number_of) if holding[i] < reach]
        mass, left = sum([loads[i] for i in candidates]), spare
        for i in candidates:
            addition = min(reach - holding[i], max(1, left * loads[i] // mass), spare)
            holding[i] = holding[i] + addition
            spare = spare - addition
    return np.array(holding)


def bell_draw(stream_key, dims, deviation, bound, shards=(), kind=jnp.bfloat16):
    result = deviation * jax.random.normal(stream_key, dims, jnp.float32)
    if shards:
        result = result * block_scale(stream_key, dims, shards, -0.22, 0.18)
    return jnp.clip(result, -bound, bound).astype(kind)


def setup_inputs(seed: int = 0) -> dict:
    splits = jax.random.split(jax.random.key(seed), 14)
    resid_in = bell_draw(splits[0], (TOKENS, D), 1.0, 6.0, ((0, 32),))
    queries = draw_queries(jax.random.fold_in(splits[13], 71), 0)
    fresh_kv = draw_fresh_kv(jax.random.fold_in(splits[13], 71), 0)
    kv_pool = bell_draw(splits[3], (N_REQ, N_EXP, PAGES_DEV, PAGE, KVW), 1.0, 6.0, ((0, 8), (1, 4)))
    block_table = draw_block_table(jax.random.fold_in(splits[13], 71), 0)
    lengths = draw_lengths(jax.random.fold_in(splits[13], 71), 0)
    mig_source = draw_mig_source(jax.random.fold_in(splits[13], 71), 0)
    mig_target = draw_mig_target(jax.random.fold_in(splits[13], 71), 0)
    expert_ids_keys = jax.random.split(jax.random.fold_in(splits[8], 1), TOKENS // (N_EXP * TOK))
    expert_ids_turns = jax.random.permutation(jax.random.fold_in(splits[8], 3), TOKENS // (N_EXP * TOK))
    expert_ids = jax.vmap(lambda own, number: routed_block(jax.random.fold_in(splits[8], 2), own, number, N_EXP * TOK, EXPERTS, TOPK, CAP, 1))(expert_ids_keys, expert_ids_turns).reshape((TOKENS, TOPK))
    gate_values = jnp.clip(0.2 + 0.8 * jax.random.uniform(splits[9], (TOKENS, TOPK), jnp.float32) ** block_scale(splits[9], (TOKENS, TOPK), ((0, 8),), -0.2, 0.2), 0.2, 1.0)
    norm_gain = jnp.clip(1.0 + 0.1 * jax.random.normal(splits[10], (D,), jnp.float32), 0.5, 1.5).astype(jnp.bfloat16)
    w_in = bell_draw(splits[11], (N_EXP, N_REQ, D, FH), D ** -0.5, 0.09375, ((0, 4), (1, 8)))
    w_out = bell_draw(splits[12], (N_EXP, N_REQ, FH, D), FF ** -0.5, 0.125, ((0, 4), (1, 8)))
    return dict(resid_in=resid_in, queries=queries, fresh_kv=fresh_kv, kv_pool=kv_pool, block_table=block_table, lengths=lengths, mig_source=mig_source, mig_target=mig_target, expert_ids=expert_ids, gate_values=gate_values, norm_gain=norm_gain, w_in=w_in, w_out=w_out)


neg_big = -1e+30
norm_eps = 1e-06

def pick_pages(pool_pages, page_ids):
    return jax.vmap(jax.vmap(lambda device_pages, device_ids: device_pages[device_ids]))(pool_pages, page_ids)

def migrate(kv_pool, mig_source, mig_target):
    to_next = pick_pages(kv_pool, mig_source[:, :, 0])
    to_prev = pick_pages(kv_pool, mig_source[:, :, 1])
    arrived = jnp.concatenate([jnp.roll(to_next, 1, axis=0), jnp.roll(to_prev, -1, axis=0)], axis=2)
    targets = jnp.concatenate([mig_target[:, :, 0], mig_target[:, :, 1]], axis=2)
    return jax.vmap(jax.vmap(lambda device_pages, device_ids, incoming: device_pages.at[device_ids].set(incoming)))(kv_pool, targets, arrived)

def attend_device(packed):
    pages, table, request_lengths, query_rows, fresh_rows = packed
    group_size = HEADS // KV_HEADS
    key_width = KV_HEADS * HEAD_DIM
    span = CTX + DRAFT
    cache = pages[table].reshape(REQ_DEV, CTX, KVW)
    stacked = jnp.concatenate([cache, fresh_rows.reshape(REQ_DEV, DRAFT, KVW)], axis=1).astype(jnp.float32)
    key_part = stacked[:, :, :key_width].reshape(REQ_DEV, span, KV_HEADS, HEAD_DIM)
    value_part = stacked[:, :, key_width:].reshape(REQ_DEV, span, KV_HEADS, HEAD_DIM)
    query_part = query_rows.astype(jnp.float32).reshape(REQ_DEV, DRAFT, KV_HEADS, group_size, HEAD_DIM)
    scores = jnp.einsum('rdkgh,rpkh->rdkgp', query_part, key_part, precision=lax.Precision.HIGHEST) * HEAD_DIM ** (-0.5)
    position = jnp.arange(span)
    draft_index = jnp.arange(DRAFT)
    in_cache = position[None, None, :] < request_lengths[:, None, None]
    in_draft = (position[None, :] >= CTX) & (position[None, :] - CTX <= draft_index[:, None])
    visible = jnp.where(position[None, None, :] < CTX, in_cache, in_draft[None, :, :])
    live = visible[:, :, None, None, :]
    scores = jnp.where(live, scores, neg_big)
    highest = lax.optimization_barrier(jnp.max(scores, axis=-1, keepdims=True))
    weights = jnp.where(live, jnp.exp(scores - highest), 0.0)
    weight_sum = lax.optimization_barrier(jnp.sum(weights, axis=-1))
    summed = jnp.einsum('rdkgp,rpkh->rdkgh', weights, value_part, precision=lax.Precision.HIGHEST)
    return (summed / weight_sum[..., None]).reshape(TOK, HEADS * HEAD_DIM)

def reference(resid_in, queries, fresh_kv, kv_pool, block_table, lengths, mig_source, mig_target, expert_ids, gate_values, norm_gain, w_in, w_out):
    device_count = N_REQ * N_EXP
    pool_after = migrate(kv_pool, mig_source, mig_target)
    attention = lax.map(attend_device, (pool_after.reshape(device_count, PAGES_DEV, PAGE, KVW), block_table.reshape(device_count, REQ_DEV, MAXP), lengths.reshape(device_count, REQ_DEV), queries.reshape(device_count, TOK, D), fresh_kv.reshape(device_count, TOK, KVW)))
    residual = resid_in.astype(jnp.float32) + attention.reshape(TOKENS, D)
    inv_rms = lax.rsqrt(lax.optimization_barrier(jnp.mean(residual * residual, axis=1, keepdims=True)) + norm_eps)
    normed = (residual * inv_rms * norm_gain.astype(jnp.float32)).astype(jnp.bfloat16)
    inner_all = w_in.reshape(EXPERTS, GRP, D, FH)
    outer_all = w_out.reshape(EXPERTS, GRP, FH, D)
    limit_rows = N_REQ * CAP

    def one_expert(running, packed):
        inner_weights, outer_weights, expert = packed
        matches = expert_ids == expert
        named_rows = jnp.any(matches, axis=1)
        gate_weight = lax.optimization_barrier(jnp.sum(jnp.where(matches, gate_values, 0.0), axis=1))
        row_index = jnp.nonzero(named_rows, size=limit_rows, fill_value=0)[0].astype(jnp.int32)
        is_valid = jnp.arange(limit_rows) < jnp.sum(named_rows.astype(jnp.int32))
        inputs = normed[row_index].astype(jnp.float32)
        hidden = jnp.einsum('td,sdf->stf', inputs, inner_weights.astype(jnp.float32), precision=lax.Precision.HIGHEST)
        activated = lax.optimization_barrier(jax.nn.silu(hidden).astype(jnp.bfloat16)).astype(jnp.float32)
        partials = jnp.einsum('stf,sfd->std', activated, outer_weights.astype(jnp.float32), precision=lax.Precision.HIGHEST)
        partials = lax.optimization_barrier(partials.astype(jnp.bfloat16)).astype(jnp.float32)
        combined = lax.optimization_barrier(jnp.sum(partials, axis=0)) * jnp.where(is_valid, gate_weight[row_index], 0.0)[:, None]
        return (running.at[row_index].add(combined), None)
    expert_mix, unused = lax.scan(one_expert, jnp.zeros((TOKENS, D), jnp.float32), (inner_all, outer_all, jnp.arange(EXPERTS, dtype=jnp.int32)))
    return (residual + expert_mix).astype(jnp.bfloat16)
```

```python
import jax
import jax.numpy as jnp
from jax import lax
from jax.sharding import PartitionSpec as P

HEADS = 28
KV_HEADS = 4
HEAD_DIM = 128
EXP_DEV = 4
CAP = 24


neg_big = -1e30
norm_eps = 1e-06


def partner_steps(count):
    if count & (count - 1):
        raise ValueError("axis size")
    return [[i ^ k for i in range(count)] for k in range(1, count)]


def partner_of(index, steps):
    table = jnp.array([list(range(len(steps[0])))] + steps, dtype=jnp.int32)
    return table[:, index]


def ring_pages(block, axis, up):
    count = lax.axis_size(axis)
    pairs = [(i, (i + 1) % count) for i in range(count)]
    if not up:
        pairs = [(target, source) for source, target in pairs]
    return lax.ppermute(block, axis, pairs)


def swap_plane(block, step, group_size):
    pairs = [(q * group_size + g, p * group_size + g) for q, p in enumerate(step) for g in range(group_size)]
    return lax.ppermute(block, "req", pairs)


def swap_group(block, step, group_size):
    pairs = [(q * group_size + g, q * group_size + p) for q in range(EXP_DEV) for g, p in enumerate(step)]
    return lax.ppermute(block, "req", pairs)


def swap_exp(block, step):
    return lax.ppermute(block, "exp", list(enumerate(step)))


def partial_attention(query_grid, key_rows, visible):
    request_count = key_rows.shape[0]
    span = key_rows.shape[1]
    key_width = KV_HEADS * HEAD_DIM
    key_part = key_rows[:, :, :key_width].reshape(request_count, span, KV_HEADS, HEAD_DIM)
    value_part = (
        key_rows[:, :, key_width:]
        .reshape(request_count, span, KV_HEADS, HEAD_DIM)
        .astype(jnp.float32)
    )
    scores = jnp.einsum(
        "rdkgh,rpkh->rdkgp", query_grid, key_part, preferred_element_type=jnp.float32
    ) * HEAD_DIM ** (-0.5)
    live = visible[:, :, None, None, :]
    scores = jnp.where(live, scores, neg_big)
    highest = jnp.max(scores, axis=-1)
    weights = jnp.where(live, jnp.exp(scores - highest[..., None]), 0.0)
    weight_sum = jnp.sum(weights, axis=-1)
    summed = jnp.einsum("rdkgp,rpkh->rdkgh", weights, value_part, precision=lax.Precision.HIGHEST)
    return (highest, weight_sum, summed)


def body(
    resid_in,
    queries,
    fresh_kv,
    kv_pool,
    block_table,
    lengths,
    mig_source,
    mig_target,
    expert_ids,
    gate_values,
    norm_gain,
    w_in,
    w_out,
):
    request_count = block_table.shape[0]
    table_width = block_table.shape[1]
    page_tokens = kv_pool.shape[3]
    kv_width = kv_pool.shape[4]
    cache_span = table_width * page_tokens
    token_count = resid_in.shape[0]
    draft_count = token_count // request_count
    model_width = resid_in.shape[1]
    exp_count = lax.axis_size("exp")
    group_size = lax.axis_size("req") // EXP_DEV
    plane_steps = partner_steps(EXP_DEV)
    group_steps = partner_steps(group_size)
    exp_steps = partner_steps(exp_count)

    pool_pages = kv_pool[0, 0]
    sources = mig_source[0, 0]
    target_pairs = mig_target[0, 0]
    from_low = ring_pages(pool_pages[sources[0]], "req", True)
    from_high = ring_pages(pool_pages[sources[1]], "req", False)
    arrivals = jnp.concatenate([from_low, from_high], axis=0)
    targets = jnp.concatenate([target_pairs[0], target_pairs[1]], axis=0)

    query_grid = queries.reshape(request_count, draft_count, KV_HEADS, HEADS // KV_HEADS, HEAD_DIM)
    fresh_rows = fresh_kv.reshape(request_count, draft_count, kv_width)
    position = jnp.arange(cache_span)
    cache_visible = jnp.broadcast_to(
        position[None, None, :] < lengths[:, None, None], (request_count, draft_count, cache_span)
    )
    draft_index = jnp.arange(draft_count)
    draft_visible = jnp.broadcast_to(
        draft_index[None, :] <= draft_index[:, None], (request_count, draft_count, draft_count)
    )
    pool_after = pool_pages.at[targets].set(arrivals)
    cache_rows = pool_after[block_table].reshape(request_count, cache_span, kv_width)
    parts = partial_attention(
        query_grid,
        jnp.concatenate([cache_rows, fresh_rows], axis=1),
        jnp.concatenate([cache_visible, draft_visible], axis=2),
    )
    attention = (parts[2] / parts[1][..., None]).reshape(token_count, model_width)
    residual = resid_in.astype(jnp.float32) + attention
    inv_rms = lax.rsqrt(jnp.mean(residual * residual, axis=1, keepdims=True) + norm_eps)
    normed = (residual * inv_rms * norm_gain.astype(jnp.float32)).astype(jnp.bfloat16)

    exp_order = partner_of(lax.axis_index("exp"), exp_steps)
    plane_order = partner_of(lax.axis_index("req") // group_size, plane_steps)
    ids = expert_ids.reshape(exp_count, token_count, -1)[exp_order].reshape(expert_ids.shape)
    gates = gate_values.reshape(exp_count, token_count, -1)[exp_order].reshape(gate_values.shape)
    local_ids = lax.axis_index("exp") * EXP_DEV + plane_order
    matches = ids[None, :, :] == local_ids[:, None, None]
    is_named = jnp.any(matches, axis=2)
    gate_local = jnp.sum(jnp.where(matches, gates[None, :, :], 0.0), axis=2)
    slot_index = jnp.cumsum(is_named.astype(jnp.int32), axis=1) - 1
    placement = is_named[:, None, :] & (slot_index[:, None, :] == jnp.arange(CAP)[None, :, None])
    columns = placement.astype(jnp.bfloat16)
    gate_columns = jnp.where(placement, gate_local[:, None, :], 0.0)

    gathered = jnp.concatenate([normed] + [swap_exp(normed, step) for step in exp_steps], axis=0)
    packed = jnp.einsum(
        "kct,td->kcd", columns, gathered, preferred_element_type=jnp.float32
    ).astype(jnp.bfloat16)
    mine = jnp.concatenate(
        [packed[:1]] + [swap_plane(packed[k + 1 : k + 2], step, group_size) for k, step in enumerate(plane_steps)],
        axis=0,
    ).reshape(EXP_DEV * CAP, model_width)
    inbound = jnp.concatenate([mine] + [swap_group(mine, step, group_size) for step in group_steps], axis=0)

    hidden = jnp.dot(inbound, w_in[0, 0], preferred_element_type=jnp.float32)
    activated = jax.nn.silu(hidden).astype(jnp.bfloat16)
    partials = (
        jnp.dot(activated, w_out[0, 0], preferred_element_type=jnp.float32)
        .astype(jnp.bfloat16)
        .reshape(group_size, EXP_DEV, CAP, model_width)
    )

    summed = partials[0].astype(jnp.float32)
    for k, step in enumerate(group_steps):
        summed = summed + swap_group(partials[k + 1], step, group_size).astype(jnp.float32)
    summed = summed.astype(jnp.bfloat16)
    returned = jnp.concatenate(
        [summed[:1]] + [swap_plane(summed[k + 1 : k + 2], step, group_size) for k, step in enumerate(plane_steps)],
        axis=0,
    )
    mix = jnp.einsum(
        "kct,kcd->td", gate_columns, returned.astype(jnp.float32), precision=lax.Precision.HIGHEST
    )
    blocks = mix.reshape(exp_count, token_count, model_width)
    result = residual + blocks[0]
    blocks = blocks.astype(jnp.bfloat16)
    for k, step in enumerate(exp_steps):
        result = result + swap_exp(blocks[k + 1], step).astype(jnp.float32)
    return result.astype(jnp.bfloat16)


def solution(mesh):
    placed = (
        P(("req", "exp"), None),
        P(("req", "exp"), None),
        P(("req", "exp"), None),
        P("req", "exp", None, None, None),
        P(("req", "exp"), None),
        P(("req", "exp")),
        P("req", "exp", None, None),
        P("req", "exp", None, None),
        P("req", None),
        P("req", None),
        P(),
        P("exp", "req", None, None),
        P("exp", "req", None, None),
    )
    return jax.shard_map(
        body, mesh=mesh, in_specs=placed, out_specs=P(("req", "exp"), None), check_vma=False
    )
```

```python
import jax
import jax.numpy as jnp
from jax import lax
from jax.experimental import pallas as pl
from jax.experimental.pallas import tpu as pltpu
from jax.sharding import PartitionSpec as P

HEADS = 28
KV_HEADS = 4
HEAD_DIM = 128
EXP_DEV = 4
CAP = 24


neg_big = -1e30
norm_eps = 1e-06


def partner_steps(count):
    if count & (count - 1):
        raise ValueError("axis size")
    return [[i ^ k for i in range(count)] for k in range(1, count)]


def partner_of(index, steps):
    return index ^ jnp.arange(len(steps) + 1, dtype=jnp.int32)


def ring_pages(block, axis, up):
    count = lax.axis_size(axis)
    pairs = [(i, (i + 1) % count) for i in range(count)]
    if not up:
        pairs = [(target, source) for source, target in pairs]
    return lax.ppermute(block, axis, pairs)


def swap_plane(block, step, group_size):
    pairs = [(q * group_size + g, p * group_size + g) for q, p in enumerate(step) for g in range(group_size)]
    return lax.ppermute(block, "req", pairs)


def swap_group(block, step, group_size):
    pairs = [(q * group_size + g, q * group_size + p) for q in range(EXP_DEV) for g, p in enumerate(step)]
    return lax.ppermute(block, "req", pairs)


def swap_exp(block, step):
    return lax.ppermute(block, "exp", list(enumerate(step)))


def send_pages_kernel(source_ref, pool_ref, up_ref, down_ref):
    for side, out_ref in enumerate((up_ref, down_ref)):
        for i in range(out_ref.shape[0]):
            out_ref[i] = pool_ref[source_ref[side, i]]


def send_pages(pool_pages, sources):
    pages = jax.ShapeDtypeStruct((sources.shape[1],) + pool_pages.shape[1:], pool_pages.dtype)
    return pl.pallas_call(
        send_pages_kernel,
        out_shape=(pages, pages),
        in_specs=[pl.BlockSpec(memory_space=pltpu.SMEM), pl.BlockSpec(memory_space=pltpu.VMEM)],
        out_specs=(pl.BlockSpec(memory_space=pltpu.VMEM),) * 2,
        compiler_params=pltpu.CompilerParams(vmem_limit_bytes=4 * 1024 * 1024),
        cost_estimate=pl.CostEstimate(
            flops=4 * 1024 * 1024 * 1024, bytes_accessed=pool_pages.size * pool_pages.dtype.itemsize, transcendentals=0
        ),
        name="send_pages",
    )(sources, pool_pages)


def weighted_values(weights, values):
    high = weights.astype(jnp.bfloat16)
    low = (weights - high.astype(jnp.float32)).astype(jnp.bfloat16)
    both = jnp.dot(
        jnp.concatenate([high, low], axis=0), values, preferred_element_type=jnp.float32
    )
    return both[: weights.shape[0]] + both[weights.shape[0] :]


def local_attention_kernel(
    table_ref, length_ref, target_ref, queries_ref, fresh_ref, pool_ref, max_ref, sum_ref, out_ref, query_ref, bias_ref
):
    request_count, table_width = table_ref.shape
    token_count, kv_width = fresh_ref.shape
    moved = target_ref.shape[1]
    page_tokens = pool_ref.shape[1]
    span = table_width * page_tokens
    draft_count = token_count // request_count
    share = HEADS // KV_HEADS
    rows_count = share * token_count
    tail = HEAD_DIM
    query = queries_ref[...].astype(jnp.float32)
    fresh = jnp.concatenate(
        [
            fresh_ref[...].astype(jnp.float32),
            jnp.zeros((tail - token_count, kv_width), jnp.float32),
        ],
        axis=0,
    ).astype(fresh_ref.dtype)
    pages = [table_ref[n, i] for n in range(request_count) for i in range(table_width)]

    def cache(first):
        rows = [pool_ref[page, :, first : first + HEAD_DIM] for page in pages]
        return jnp.concatenate(rows + [fresh[:, first : first + HEAD_DIM]], axis=0)

    token = lax.broadcasted_iota(jnp.int32, (rows_count, span), 0) % token_count
    lane = lax.broadcasted_iota(jnp.int32, (rows_count, span), 1)
    live = []
    for n in range(request_count):
        arrives = (table_ref[n, 0] == target_ref[0, 0]) | (table_ref[n, 0] == target_ref[1, 0])
        first = jnp.where(arrives, moved * page_tokens, 0)
        live.append((token // draft_count == n) & (lane >= first) & (lane < length_ref[n]))
    tail_token = lax.broadcasted_iota(jnp.int32, (rows_count, tail), 0) % token_count
    tail_lane = lax.broadcasted_iota(jnp.int32, (rows_count, tail), 1)
    live.append((tail_token // draft_count == tail_lane // draft_count) & (tail_lane <= tail_token))
    live = jnp.concatenate([jnp.where(mask, 0.0, neg_big) for mask in live], axis=1)
    key_width = KV_HEADS * HEAD_DIM
    for j in range(KV_HEADS):
        heads = range(j * share, (j + 1) * share)
        rows = jnp.concatenate([query[:, h * HEAD_DIM : (h + 1) * HEAD_DIM] for h in heads], axis=0)
        query_ref[j] = rows
        scores = lax.dot_general(
            rows.astype(jnp.bfloat16), cache(j * HEAD_DIM), (((1,), (1,)), ((), ())),
            preferred_element_type=jnp.float32,
        )
        scores = jnp.where(live < 0, neg_big, scores * HEAD_DIM ** (-0.5))
        highest = jnp.max(scores, axis=1, keepdims=True)
        weights = jnp.exp(scores - highest)
        max_ref[j] = jnp.broadcast_to(highest, max_ref.shape[1:])
        sum_ref[j] = jnp.broadcast_to(jnp.sum(weights, axis=1, keepdims=True), sum_ref.shape[1:])
        out_ref[j] = weighted_values(weights, cache(key_width + j * HEAD_DIM))

    moved_span = moved * page_tokens
    token = lax.broadcasted_iota(jnp.int32, (rows_count, 2 * moved_span), 0) % token_count
    lane = lax.broadcasted_iota(jnp.int32, (rows_count, 2 * moved_span), 1)
    seen = jnp.zeros((rows_count, 2 * moved_span), jnp.float32)
    for side in range(2):
        position = lane - side * moved_span
        for n in range(request_count):
            bound = jnp.where(table_ref[n, 0] == target_ref[side, 0], length_ref[n], 0)
            inside = (position >= 0) & (position < moved_span) & (position < bound)
            seen = seen + jnp.where((token // draft_count == n) & inside, 1.0, 0.0)
    bias_ref[...] = jnp.where(seen > 0, 0.0, neg_big)


def local_attention(table, lengths, targets, queries, fresh_kv, pool_pages):
    token_count = queries.shape[0]
    moved = targets.shape[1]
    part = jax.ShapeDtypeStruct((KV_HEADS, HEADS // KV_HEADS * token_count, HEAD_DIM), jnp.float32)
    bias = jax.ShapeDtypeStruct((part.shape[1], 2 * moved * pool_pages.shape[1]), jnp.float32)
    return pl.pallas_call(
        local_attention_kernel,
        out_shape=(part, part, part, part, bias),
        in_specs=[pl.BlockSpec(memory_space=pltpu.SMEM)] * 3 + [pl.BlockSpec(memory_space=pltpu.VMEM)] * 3,
        out_specs=(pl.BlockSpec(memory_space=pltpu.VMEM),) * 5,
        compiler_params=pltpu.CompilerParams(vmem_limit_bytes=6 * 1024 * 1024),
        cost_estimate=pl.CostEstimate(flops=40 * 1024 * 1024, bytes_accessed=2 * 1024 * 1024, transcendentals=160 * 1024),
        name="local_attention",
    )(table, lengths, targets, queries, fresh_kv, pool_pages)


def arrived_attention_kernel(
    resid_ref, gain_ref, low_ref, high_ref, max_ref, sum_ref, out_ref, query_ref, bias_ref, residual_ref, normed_ref
):
    token_count, model_width = residual_ref.shape
    share = HEADS // KV_HEADS
    key_width = KV_HEADS * HEAD_DIM
    heads = range(KV_HEADS)

    def arrived(first):
        at = pl.ds(first, HEAD_DIM)
        return jnp.concatenate([low_ref[:, at], high_ref[:, at]], axis=0)

    scores = [
        lax.dot_general(
            query_ref[j].astype(jnp.bfloat16), arrived(j * HEAD_DIM), (((1,), (1,)), ((), ())),
            preferred_element_type=jnp.float32,
        )
        for j in heads
    ]
    hidden = bias_ref[...] < 0
    scores = [jnp.where(hidden, neg_big, part * HEAD_DIM ** (-0.5)) for part in scores]
    highest = [jnp.maximum(max_ref[j], jnp.max(scores[j], axis=1, keepdims=True)) for j in heads]
    weights = [jnp.exp(scores[j] - highest[j][:, :1]) for j in heads]
    scale = [jnp.exp(max_ref[j] - highest[j]) for j in heads]
    total = [sum_ref[j] * scale[j] + jnp.sum(weights[j], axis=1, keepdims=True) for j in heads]
    summed = [
        out_ref[j] * scale[j] + weighted_values(weights[j], arrived(key_width + j * HEAD_DIM)) for j in heads
    ]
    blocks = []
    for j in heads:
        attention = summed[j] / total[j]
        for h in range(share):
            first = (j * share + h) * HEAD_DIM
            resid = resid_ref[:, first : first + HEAD_DIM].astype(jnp.float32)
            blocks.append(resid + attention[h * token_count : (h + 1) * token_count])
    squares = blocks[0] * blocks[0]
    for block in blocks[1:]:
        squares = squares + block * block
    inv_rms = lax.rsqrt(jnp.sum(squares, axis=1, keepdims=True) / model_width + norm_eps)
    residual = jnp.concatenate(blocks, axis=1)
    residual_ref[...] = residual
    normed_ref[...] = (residual * inv_rms * gain_ref[...].astype(jnp.float32)[None, :]).astype(normed_ref.dtype)


def arrived_attention(resid_in, gain, low, high, parts):
    shape = resid_in.shape
    return pl.pallas_call(
        arrived_attention_kernel,
        out_shape=(jax.ShapeDtypeStruct(shape, jnp.float32), jax.ShapeDtypeStruct(shape, jnp.bfloat16)),
        in_specs=[pl.BlockSpec(memory_space=pltpu.VMEM)] * 9,
        out_specs=(pl.BlockSpec(memory_space=pltpu.VMEM),) * 2,
        compiler_params=pltpu.CompilerParams(vmem_limit_bytes=4 * 1024 * 1024),
        cost_estimate=pl.CostEstimate(flops=8 * 1024 * 1024 * 1024, bytes_accessed=2 * 1024 * 1024, transcendentals=60 * 1024),
        name="arrived_attention",
    )(resid_in, gain, low, high, *parts)


def load_kernel(weight_ref, out_ref, sem):
    copy = pltpu.make_async_copy(weight_ref, out_ref, sem)
    copy.start()
    copy.wait()


def load(weight):
    return pl.pallas_call(
        load_kernel,
        out_shape=jax.ShapeDtypeStruct(weight.shape, weight.dtype),
        in_specs=[pl.BlockSpec(memory_space=pltpu.HBM)],
        out_specs=pl.BlockSpec(memory_space=pltpu.VMEM),
        scratch_shapes=[pltpu.SemaphoreType.DMA],
        compiler_params=pltpu.CompilerParams(vmem_limit_bytes=1024 * 1024),
        cost_estimate=pl.CostEstimate(
            flops=0, bytes_accessed=2 * weight.size * weight.dtype.itemsize, transcendentals=0
        ),
        name="load_weight",
    )(weight)


def body(
    resid_in,
    queries,
    fresh_kv,
    kv_pool,
    block_table,
    lengths,
    mig_source,
    mig_target,
    expert_ids,
    gate_values,
    norm_gain,
    w_in,
    w_out,
):
    token_count = resid_in.shape[0]
    model_width = resid_in.shape[1]
    exp_count = lax.axis_size("exp")
    group_size = lax.axis_size("req") // EXP_DEV
    plane_steps = partner_steps(EXP_DEV)
    group_steps = partner_steps(group_size)
    exp_steps = partner_steps(exp_count)

    pool_pages = kv_pool[0, 0]
    targets = mig_target[0, 0]
    up, down = send_pages(pool_pages, mig_source[0, 0])
    moved_shape = (up.shape[0] * up.shape[1], up.shape[2])
    from_low = ring_pages(up.reshape(moved_shape), "req", True)
    from_high = ring_pages(down.reshape(moved_shape), "req", False)

    parts = local_attention(block_table, lengths, targets, queries, fresh_kv, pool_pages)
    residual, normed = arrived_attention(resid_in, norm_gain, from_low, from_high, parts)
    normed, expert_ids, gate_values, inner = lax.optimization_barrier(
        (normed, expert_ids, gate_values, w_in[0, 0])
    )

    exp_order = partner_of(lax.axis_index("exp"), exp_steps)
    plane_order = partner_of(lax.axis_index("req") // group_size, plane_steps)
    ids = expert_ids.reshape(exp_count, token_count, -1)[exp_order].reshape(expert_ids.shape)
    gates = gate_values.reshape(exp_count, token_count, -1)[exp_order].reshape(gate_values.shape)
    local_ids = lax.axis_index("exp") * EXP_DEV + plane_order
    matches = ids[None, :, :] == local_ids[:, None, None]
    is_named = jnp.any(matches, axis=2)
    gate_local = jnp.sum(jnp.where(matches, gates[None, :, :], 0.0), axis=2)
    slot_index = jnp.cumsum(is_named.astype(jnp.int32), axis=1) - 1
    placement = is_named[:, None, :] & (slot_index[:, None, :] == jnp.arange(CAP)[None, :, None])
    columns = placement.astype(jnp.bfloat16)
    gate_columns = jnp.where(placement, gate_local[:, None, :], 0.0)

    gathered = jnp.concatenate([normed] + [swap_exp(normed, step) for step in exp_steps], axis=0)
    packed = jnp.einsum(
        "kct,td->kcd", columns, gathered, preferred_element_type=jnp.float32
    ).astype(jnp.bfloat16)
    packed, outer = lax.optimization_barrier((packed, w_out[0, 0]))
    inner = load(inner)
    outer = load(outer)
    pieces = [packed[0]] + [
        swap_plane(packed[k + 1], step, group_size) for k, step in enumerate(plane_steps)
    ]
    inbound = jnp.concatenate(
        pieces + [swap_group(piece, step, group_size) for step in group_steps for piece in pieces], axis=0
    )

    hidden = lax.optimization_barrier(jnp.dot(inbound, inner, preferred_element_type=jnp.float32))
    activated = lax.optimization_barrier(jax.nn.silu(hidden).astype(jnp.bfloat16))

    def outer_rows(rows):
        return jnp.dot(rows, outer, preferred_element_type=jnp.float32)

    share = EXP_DEV * CAP
    others = outer_rows(activated[share:]).astype(jnp.bfloat16)
    arrived = [
        swap_group(others[k * share : (k + 1) * share], step, group_size) for k, step in enumerate(group_steps)
    ]
    activated, others = lax.optimization_barrier((activated, others))
    summed = lax.optimization_barrier(outer_rows(activated[:share]))
    for part in arrived:
        summed = summed + part.astype(jnp.float32)
    summed = summed.astype(jnp.bfloat16).reshape(EXP_DEV, CAP, model_width)

    returned = jnp.concatenate(
        [summed[:1]] + [swap_plane(summed[k + 1 : k + 2], step, group_size) for k, step in enumerate(plane_steps)],
        axis=0,
    )
    mix = jnp.einsum(
        "kct,kcd->td", gate_columns, returned.astype(jnp.float32), precision=lax.Precision.HIGHEST
    )
    blocks = mix.reshape(exp_count, token_count, model_width)
    result = residual + blocks[0]
    blocks = blocks.astype(jnp.bfloat16)
    for k, step in enumerate(exp_steps):
        result = result + swap_exp(blocks[k + 1], step).astype(jnp.float32)
    return result.astype(jnp.bfloat16)


def solution(mesh):
    placed = (
        P(("req", "exp"), None),
        P(("req", "exp"), None),
        P(("req", "exp"), None),
        P("req", "exp", None, None, None),
        P(("req", "exp"), None),
        P(("req", "exp")),
        P("req", "exp", None, None),
        P("req", "exp", None, None),
        P("req", None),
        P("req", None),
        P(),
        P("exp", "req", None, None),
        P("exp", "req", None, None),
    )
    return jax.shard_map(
        body, mesh=mesh, in_specs=placed, out_specs=P(("req", "exp"), None), check_vma=False
    )
```

```python
import jax
import jax.numpy as jnp
from jax import lax
from jax.experimental import pallas as pl
from jax.experimental.pallas import tpu as pltpu
from jax.sharding import PartitionSpec as P

HEADS = 28
KV_HEADS = 4
HEAD_DIM = 128
EXP_DEV = 4
CAP = 24


neg_big = -1e30
norm_eps = 1e-06


def partner_steps(count):
    if count & (count - 1):
        raise ValueError("axis size")
    return [[i ^ k for i in range(count)] for k in range(1, count)]


def partner_of(index, steps):
    return index ^ jnp.array([0] + [step[0] for step in steps], dtype=jnp.int32)


def ring_pages(block, axis, up):
    count = lax.axis_size(axis)
    pairs = [(i, (i + 1) % count) for i in range(count)]
    if not up:
        pairs = [(target, source) for source, target in pairs]
    return lax.ppermute(block, axis, pairs)


def swap_plane(block, step, group_size):
    pairs = [(q * group_size + g, p * group_size + g) for q, p in enumerate(step) for g in range(group_size)]
    return lax.ppermute(block, "req", pairs)


def swap_group(block, step, group_size):
    pairs = [(q * group_size + g, q * group_size + p) for q in range(EXP_DEV) for g, p in enumerate(step)]
    return lax.ppermute(block, "req", pairs)


def swap_exp(block, step):
    return lax.ppermute(block, "exp", list(enumerate(step)))


def opening_kernel(out_ref):
    out_ref[...] = jnp.zeros_like(out_ref)


def opening():
    return pl.pallas_call(
        opening_kernel,
        out_shape=jax.ShapeDtypeStruct((8, HEAD_DIM), jnp.float32),
        out_specs=pl.BlockSpec(memory_space=pltpu.VMEM),
        compiler_params=pltpu.CompilerParams(vmem_limit_bytes=1024 * 1024),
        cost_estimate=pl.CostEstimate(flops=4 * 1024 * 1024 * 1024, bytes_accessed=4096, transcendentals=0),
        name="opening",
    )()


def send_pages_kernel(source_ref, pool_ref, after_ref, up_ref, down_ref):
    for side, out_ref in enumerate((up_ref, down_ref)):
        for i in range(out_ref.shape[0]):
            out_ref[i] = pool_ref[source_ref[side, i]]


def send_pages(pool_pages, sources, after):
    pages = jax.ShapeDtypeStruct((sources.shape[1],) + pool_pages.shape[1:], pool_pages.dtype)
    return pl.pallas_call(
        send_pages_kernel,
        out_shape=(pages, pages),
        in_specs=[pl.BlockSpec(memory_space=pltpu.SMEM)] + [pl.BlockSpec(memory_space=pltpu.VMEM)] * 2,
        out_specs=(pl.BlockSpec(memory_space=pltpu.VMEM),) * 2,
        compiler_params=pltpu.CompilerParams(vmem_limit_bytes=4 * 1024 * 1024),
        cost_estimate=pl.CostEstimate(
            flops=4 * 1024 * 1024 * 1024, bytes_accessed=pool_pages.size * pool_pages.dtype.itemsize, transcendentals=0
        ),
        name="send_pages",
    )(sources, pool_pages, after)


def weighted_values(weights, values):
    high = weights.astype(jnp.bfloat16)
    low = (weights - high.astype(jnp.float32)).astype(jnp.bfloat16)
    both = jnp.dot(
        jnp.concatenate([high, low], axis=0), values, preferred_element_type=jnp.float32
    )
    return both[: weights.shape[0]] + both[weights.shape[0] :]


def local_attention_kernel(
    table_ref, length_ref, target_ref, queries_ref, fresh_ref, pool_ref, max_ref, sum_ref, out_ref, query_ref, bias_ref
):
    request_count, table_width = table_ref.shape
    token_count, kv_width = fresh_ref.shape
    moved = target_ref.shape[1]
    page_tokens = pool_ref.shape[1]
    span = table_width * page_tokens
    draft_count = token_count // request_count
    share = HEADS // KV_HEADS
    rows_count = share * token_count
    tail = HEAD_DIM
    query = queries_ref[...].astype(jnp.float32)
    fresh = jnp.concatenate(
        [
            fresh_ref[...].astype(jnp.float32),
            jnp.zeros((tail - token_count, kv_width), jnp.float32),
        ],
        axis=0,
    ).astype(fresh_ref.dtype)
    pages = [table_ref[n, i] for n in range(request_count) for i in range(table_width)]

    def cache(first):
        rows = [pool_ref[page, :, first : first + HEAD_DIM] for page in pages]
        return jnp.concatenate(rows + [fresh[:, first : first + HEAD_DIM]], axis=0)

    token = lax.broadcasted_iota(jnp.int32, (rows_count, span), 0) % token_count
    lane = lax.broadcasted_iota(jnp.int32, (rows_count, span), 1)
    live = []
    for n in range(request_count):
        arrives = (table_ref[n, 0] == target_ref[0, 0]) | (table_ref[n, 0] == target_ref[1, 0])
        first = jnp.where(arrives, moved * page_tokens, 0)
        live.append((token // draft_count == n) & (lane >= first) & (lane < length_ref[n]))
    tail_token = lax.broadcasted_iota(jnp.int32, (rows_count, tail), 0) % token_count
    tail_lane = lax.broadcasted_iota(jnp.int32, (rows_count, tail), 1)
    live.append((tail_token // draft_count == tail_lane // draft_count) & (tail_lane <= tail_token))
    live = jnp.concatenate([jnp.where(mask, 0.0, neg_big) for mask in live], axis=1)
    key_width = KV_HEADS * HEAD_DIM
    for j in range(KV_HEADS):
        heads = range(j * share, (j + 1) * share)
        rows = jnp.concatenate([query[:, h * HEAD_DIM : (h + 1) * HEAD_DIM] for h in heads], axis=0)
        query_ref[j] = rows
        scores = lax.dot_general(
            rows.astype(jnp.bfloat16), cache(j * HEAD_DIM), (((1,), (1,)), ((), ())),
            preferred_element_type=jnp.float32,
        )
        scores = jnp.where(live < 0, neg_big, scores * HEAD_DIM ** (-0.5))
        highest = jnp.max(scores, axis=1, keepdims=True)
        weights = jnp.exp(scores - highest)
        max_ref[j] = jnp.broadcast_to(highest, max_ref.shape[1:])
        sum_ref[j] = jnp.broadcast_to(jnp.sum(weights, axis=1, keepdims=True), sum_ref.shape[1:])
        out_ref[j] = weighted_values(weights, cache(key_width + j * HEAD_DIM))

    moved_span = moved * page_tokens
    token = lax.broadcasted_iota(jnp.int32, (rows_count, 2 * moved_span), 0) % token_count
    lane = lax.broadcasted_iota(jnp.int32, (rows_count, 2 * moved_span), 1)
    seen = jnp.zeros((rows_count, 2 * moved_span), jnp.float32)
    for side in range(2):
        position = lane - side * moved_span
        for n in range(request_count):
            bound = jnp.where(table_ref[n, 0] == target_ref[side, 0], length_ref[n], 0)
            inside = (position >= 0) & (position < moved_span) & (position < bound)
            seen = seen + jnp.where((token // draft_count == n) & inside, 1.0, 0.0)
    bias_ref[...] = jnp.where(seen > 0, 0.0, neg_big)


def local_attention(table, lengths, targets, queries, fresh_kv, pool_pages):
    token_count = queries.shape[0]
    moved = targets.shape[1]
    part = jax.ShapeDtypeStruct((KV_HEADS, HEADS // KV_HEADS * token_count, HEAD_DIM), jnp.float32)
    bias = jax.ShapeDtypeStruct((part.shape[1], 2 * moved * pool_pages.shape[1]), jnp.float32)
    return pl.pallas_call(
        local_attention_kernel,
        out_shape=(part, part, part, part, bias),
        in_specs=[pl.BlockSpec(memory_space=pltpu.SMEM)] * 3 + [pl.BlockSpec(memory_space=pltpu.VMEM)] * 3,
        out_specs=(pl.BlockSpec(memory_space=pltpu.VMEM),) * 5,
        compiler_params=pltpu.CompilerParams(vmem_limit_bytes=6 * 1024 * 1024),
        cost_estimate=pl.CostEstimate(flops=40 * 1024 * 1024, bytes_accessed=2 * 1024 * 1024, transcendentals=160 * 1024),
        name="local_attention",
    )(table, lengths, targets, queries, fresh_kv, pool_pages)


def arrived_attention_kernel(
    resid_ref, gain_ref, low_ref, high_ref, max_ref, sum_ref, out_ref, query_ref, bias_ref, residual_ref, normed_ref
):
    token_count, model_width = residual_ref.shape
    share = HEADS // KV_HEADS
    key_width = KV_HEADS * HEAD_DIM
    heads = range(KV_HEADS)

    def arrived(first):
        at = pl.ds(first, HEAD_DIM)
        return jnp.concatenate([low_ref[:, at], high_ref[:, at]], axis=0)

    scores = [
        lax.dot_general(
            query_ref[j].astype(jnp.bfloat16), arrived(j * HEAD_DIM), (((1,), (1,)), ((), ())),
            preferred_element_type=jnp.float32,
        )
        for j in heads
    ]
    hidden = bias_ref[...] < 0
    scores = [jnp.where(hidden, neg_big, part * HEAD_DIM ** (-0.5)) for part in scores]
    highest = [jnp.maximum(max_ref[j], jnp.max(scores[j], axis=1, keepdims=True)) for j in heads]
    weights = [jnp.exp(scores[j] - highest[j][:, :1]) for j in heads]
    scale = [jnp.exp(max_ref[j] - highest[j]) for j in heads]
    total = [sum_ref[j] * scale[j] + jnp.sum(weights[j], axis=1, keepdims=True) for j in heads]
    summed = [
        out_ref[j] * scale[j] + weighted_values(weights[j], arrived(key_width + j * HEAD_DIM)) for j in heads
    ]
    blocks = []
    for j in heads:
        attention = summed[j] / total[j]
        for h in range(share):
            first = (j * share + h) * HEAD_DIM
            resid = resid_ref[:, first : first + HEAD_DIM].astype(jnp.float32)
            blocks.append(resid + attention[h * token_count : (h + 1) * token_count])
    squares = blocks[0] * blocks[0]
    for block in blocks[1:]:
        squares = squares + block * block
    inv_rms = lax.rsqrt(jnp.sum(squares, axis=1, keepdims=True) / model_width + norm_eps)
    residual = jnp.concatenate(blocks, axis=1)
    residual_ref[...] = residual
    normed_ref[...] = (residual * inv_rms * gain_ref[...].astype(jnp.float32)[None, :]).astype(normed_ref.dtype)


def arrived_attention(resid_in, gain, low, high, parts):
    shape = resid_in.shape
    return pl.pallas_call(
        arrived_attention_kernel,
        out_shape=(jax.ShapeDtypeStruct(shape, jnp.float32), jax.ShapeDtypeStruct(shape, jnp.bfloat16)),
        in_specs=[pl.BlockSpec(memory_space=pltpu.VMEM)] * 9,
        out_specs=(pl.BlockSpec(memory_space=pltpu.VMEM),) * 2,
        compiler_params=pltpu.CompilerParams(vmem_limit_bytes=4 * 1024 * 1024),
        cost_estimate=pl.CostEstimate(flops=1024 * 1024 * 1024, bytes_accessed=2 * 1024 * 1024, transcendentals=60 * 1024),
        name="arrived_attention",
    )(resid_in, gain, low, high, *parts)


def pack_kernel(columns_ref, *refs):
    out_refs = refs[-EXP_DEV:]
    rows = jnp.concatenate([ref[...].astype(jnp.float32) for ref in refs[:-EXP_DEV]], axis=0)
    slots = jnp.dot(columns_ref[...], rows.astype(jnp.bfloat16), preferred_element_type=jnp.float32)
    for k, out_ref in enumerate(out_refs):
        out_ref[...] = slots[k * CAP : (k + 1) * CAP].astype(out_ref.dtype)


def pack(columns, parts):
    slots = jax.ShapeDtypeStruct((CAP, parts[0].shape[1]), parts[0].dtype)
    return pl.pallas_call(
        pack_kernel,
        out_shape=(slots,) * EXP_DEV,
        in_specs=[pl.BlockSpec(memory_space=pltpu.VMEM)] * (1 + len(parts)),
        out_specs=(pl.BlockSpec(memory_space=pltpu.VMEM),) * EXP_DEV,
        compiler_params=pltpu.CompilerParams(vmem_limit_bytes=8 * 1024 * 1024),
        cost_estimate=pl.CostEstimate(
            flops=8 * 1024 * 1024 * 1024, bytes_accessed=2 * 1024 * 1024, transcendentals=0
        ),
        name="pack",
    )(columns.reshape(EXP_DEV * CAP, -1), *parts)


def expert_kernel(rows_ref, inner_ref, outer_ref, own_ref, others_ref):
    rows = rows_ref[...]
    own = own_ref.shape[0]
    tile = min(2 * HEAD_DIM, own_ref.shape[1])
    parts = []
    for c in range(0, own_ref.shape[1], tile):
        hidden = jnp.dot(rows, inner_ref[:, c : c + tile], preferred_element_type=jnp.float32)
        activated = (hidden / (1.0 + jnp.exp(-hidden))).astype(own_ref.dtype)
        own_ref[:, c : c + tile] = activated[:own]
        parts.append(activated[own:])
    activated = jnp.concatenate(parts, axis=1)
    tile = 2 * HEAD_DIM
    for c in range(0, others_ref.shape[1], tile):
        others_ref[:, c : c + tile] = jnp.dot(
            activated, outer_ref[:, c : c + tile], preferred_element_type=jnp.float32
        ).astype(others_ref.dtype)


def expert(rows, inner, outer, own):
    return pl.pallas_call(
        expert_kernel,
        out_shape=(
            jax.ShapeDtypeStruct((own, inner.shape[1]), rows.dtype),
            jax.ShapeDtypeStruct((rows.shape[0] - own, outer.shape[1]), rows.dtype),
        ),
        in_specs=[pl.BlockSpec(memory_space=pltpu.VMEM)] * 3,
        out_specs=(pl.BlockSpec(memory_space=pltpu.VMEM),) * 2,
        compiler_params=pltpu.CompilerParams(vmem_limit_bytes=32 * 1024 * 1024),
        cost_estimate=pl.CostEstimate(
            flops=2 * rows.shape[0] * (inner.size + outer.size),
            bytes_accessed=(inner.size + outer.size) * inner.dtype.itemsize,
            transcendentals=rows.shape[0] * inner.shape[1],
        ),
        name="expert",
    )(rows, inner, outer)


def own_rows_kernel(rows_ref, outer_ref, out_ref):
    rows = rows_ref[...]
    tile = 2 * HEAD_DIM
    for c in range(0, out_ref.shape[1], tile):
        out_ref[:, c : c + tile] = jnp.dot(rows, outer_ref[:, c : c + tile], preferred_element_type=jnp.float32)


def own_rows(rows, outer):
    return pl.pallas_call(
        own_rows_kernel,
        out_shape=jax.ShapeDtypeStruct((rows.shape[0], outer.shape[1]), jnp.float32),
        in_specs=[pl.BlockSpec(memory_space=pltpu.VMEM)] * 2,
        out_specs=pl.BlockSpec(memory_space=pltpu.VMEM),
        compiler_params=pltpu.CompilerParams(vmem_limit_bytes=16 * 1024 * 1024),
        cost_estimate=pl.CostEstimate(
            flops=2 * rows.shape[0] * outer.size,
            bytes_accessed=outer.size * outer.dtype.itemsize,
            transcendentals=0,
        ),
        name="own_rows",
    )(rows, outer)


def body(
    resid_in,
    queries,
    fresh_kv,
    kv_pool,
    block_table,
    lengths,
    mig_source,
    mig_target,
    expert_ids,
    gate_values,
    norm_gain,
    w_in,
    w_out,
):
    token_count = resid_in.shape[0]
    model_width = resid_in.shape[1]
    exp_count = lax.axis_size("exp")
    group_size = lax.axis_size("req") // EXP_DEV
    plane_steps = partner_steps(EXP_DEV)[::-1]
    group_steps = partner_steps(group_size)
    exp_steps = partner_steps(exp_count)

    pool_pages = kv_pool[0, 0]
    targets = mig_target[0, 0]
    up, down = send_pages(pool_pages, mig_source[0, 0], opening())
    moved_shape = (up.shape[0] * up.shape[1], up.shape[2])
    from_low = ring_pages(up.reshape(moved_shape), "req", True)
    from_high = ring_pages(down.reshape(moved_shape), "req", False)

    parts = local_attention(block_table, lengths, targets, queries, fresh_kv, pool_pages)
    residual, normed = arrived_attention(resid_in, norm_gain, from_low, from_high, parts)
    normed, expert_ids, gate_values = lax.optimization_barrier((normed, expert_ids, gate_values))

    exp_order = partner_of(lax.axis_index("exp"), exp_steps)
    plane_order = partner_of(lax.axis_index("req") // group_size, plane_steps)
    ids = expert_ids.reshape(exp_count, token_count, -1)[exp_order].reshape(expert_ids.shape)
    gates = gate_values.reshape(exp_count, token_count, -1)[exp_order].reshape(gate_values.shape)
    local_ids = lax.axis_index("exp") * EXP_DEV + plane_order
    matches = ids[None, :, :] == local_ids[:, None, None]
    is_named = jnp.any(matches, axis=2)
    gate_local = jnp.sum(jnp.where(matches, gates[None, :, :], 0.0), axis=2)
    slot_index = jnp.cumsum(is_named.astype(jnp.int32), axis=1) - 1
    placement = is_named[:, None, :] & (slot_index[:, None, :] == jnp.arange(CAP)[None, :, None])
    columns = placement.astype(jnp.bfloat16)
    gate_columns = jnp.where(placement, gate_local[:, None, :], 0.0)

    packed = pack(columns, [normed] + [swap_exp(normed, step) for step in exp_steps])
    pieces = [packed[0]] + [
        swap_plane(packed[k + 1], step, group_size) for k, step in enumerate(plane_steps)
    ]
    inbound = jnp.concatenate(
        pieces + [swap_group(piece, step, group_size) for step in group_steps for piece in pieces], axis=0
    )

    share = EXP_DEV * CAP
    activated, others = expert(inbound, w_in[0, 0], w_out[0, 0], share)
    arrived = [
        swap_group(others[k * share : (k + 1) * share], step, group_size) for k, step in enumerate(group_steps)
    ]
    activated, others = lax.optimization_barrier((activated, others))
    summed = own_rows(activated, w_out[0, 0])
    for part in arrived:
        summed = summed + part.astype(jnp.float32)
    summed = summed.astype(jnp.bfloat16).reshape(EXP_DEV, CAP, model_width)

    returned = jnp.concatenate(
        [summed[:1]] + [swap_plane(summed[k + 1 : k + 2], step, group_size) for k, step in enumerate(plane_steps)],
        axis=0,
    )
    mix = jnp.einsum(
        "kct,kcd->td", gate_columns, returned.astype(jnp.float32), precision=lax.Precision.HIGHEST
    )
    blocks = mix.reshape(exp_count, token_count, model_width)
    result = residual + blocks[0]
    blocks = blocks.astype(jnp.bfloat16)
    for k, step in enumerate(exp_steps):
        result = result + swap_exp(blocks[k + 1], step).astype(jnp.float32)
    return result.astype(jnp.bfloat16)


def solution(mesh):
    placed = (
        P(("req", "exp"), None),
        P(("req", "exp"), None),
        P(("req", "exp"), None),
        P("req", "exp", None, None, None),
        P(("req", "exp"), None),
        P(("req", "exp")),
        P("req", "exp", None, None),
        P("req", "exp", None, None),
        P("req", None),
        P("req", None),
        P(),
        P("exp", "req", None, None),
        P("exp", "req", None, None),
    )
    return jax.shard_map(
        body, mesh=mesh, in_specs=placed, out_specs=P(("req", "exp"), None), check_vma=False
    )
```

```python
import jax
import jax.numpy as jnp
from jax import lax
from jax.experimental import pallas as pl
from jax.experimental.pallas import tpu as pltpu
from jax.sharding import PartitionSpec as P

HEADS = 28
KV_HEADS = 4
HEAD_DIM = 128
EXP_DEV = 4
CAP = 24
PLANE_ORDERS = ((2, 3, 1), (1, 3, 2))


neg_big = -1e30
norm_eps = 1e-06


def partner_steps(count):
    if count & (count - 1):
        raise ValueError("axis size")
    return [[i ^ k for i in range(count)] for k in range(1, count)]


def partner_of(index, orders, member):
    return index ^ jnp.array([[0] + list(order) for order in orders], dtype=jnp.int32)[member % len(orders)]


def swap_ring(block, offset):
    count = lax.axis_size("req")
    if count % 2:
        raise ValueError("axis size")
    pairs = []
    for i in range(offset, count, 2):
        pairs += [(i, (i + 1) % count), ((i + 1) % count, i)]
    return lax.ppermute(block, "req", pairs)


def swap_plane(block, k, orders, group_size):
    pairs = [
        (q * group_size + g, (q ^ orders[g % len(orders)][k]) * group_size + g)
        for q in range(EXP_DEV)
        for g in range(group_size)
    ]
    return lax.ppermute(block, "req", pairs)


def swap_group(block, step, group_size):
    pairs = [(q * group_size + g, q * group_size + p) for q in range(EXP_DEV) for g, p in enumerate(step)]
    return lax.ppermute(block, "req", pairs)


def swap_exp(block, k, orders, group_size):
    count = lax.axis_size("exp")
    pairs = [
        (r * count + e, r * count + (e ^ orders[r % group_size % len(orders)][k]))
        for r in range(lax.axis_size("req"))
        for e in range(count)
    ]
    return lax.ppermute(block, ("req", "exp"), pairs)


def opening_kernel(out_ref):
    out_ref[...] = jnp.zeros_like(out_ref)


def opening():
    return pl.pallas_call(
        opening_kernel,
        out_shape=jax.ShapeDtypeStruct((8, HEAD_DIM), jnp.float32),
        out_specs=pl.BlockSpec(memory_space=pltpu.VMEM),
        compiler_params=pltpu.CompilerParams(vmem_limit_bytes=1024 * 1024),
        cost_estimate=pl.CostEstimate(flops=4 * 1024 * 1024 * 1024, bytes_accessed=4096, transcendentals=0),
        name="opening",
    )()


def send_pages_kernel(source_ref, pool_ref, after_ref, far_ref, near_ref):
    odd = lax.rem(lax.axis_index("req"), 2)
    for side, out_ref in ((1 - odd, far_ref), (odd, near_ref)):
        for i in range(out_ref.shape[0]):
            out_ref[i] = pool_ref[source_ref[side, i]]


def send_pages(pool_pages, sources, after):
    pages = jax.ShapeDtypeStruct((sources.shape[1],) + pool_pages.shape[1:], pool_pages.dtype)
    return pl.pallas_call(
        send_pages_kernel,
        out_shape=(pages, pages),
        in_specs=[pl.BlockSpec(memory_space=pltpu.SMEM)] + [pl.BlockSpec(memory_space=pltpu.VMEM)] * 2,
        out_specs=(pl.BlockSpec(memory_space=pltpu.VMEM),) * 2,
        compiler_params=pltpu.CompilerParams(vmem_limit_bytes=4 * 1024 * 1024),
        cost_estimate=pl.CostEstimate(
            flops=4 * 1024 * 1024 * 1024, bytes_accessed=pool_pages.size * pool_pages.dtype.itemsize, transcendentals=0
        ),
        name="send_pages",
    )(sources, pool_pages, after)


def weighted_values(weights, values):
    high = weights.astype(jnp.bfloat16)
    low = (weights - high.astype(jnp.float32)).astype(jnp.bfloat16)
    both = jnp.dot(
        jnp.concatenate([high, low], axis=0), values, preferred_element_type=jnp.float32
    )
    return both[: weights.shape[0]] + both[weights.shape[0] :]


def local_attention_kernel(
    table_ref, length_ref, target_ref, queries_ref, fresh_ref, pool_ref, max_ref, sum_ref, out_ref, query_ref, bias_ref
):
    request_count, table_width = table_ref.shape
    token_count, kv_width = fresh_ref.shape
    moved = target_ref.shape[1]
    page_tokens = pool_ref.shape[1]
    span = table_width * page_tokens
    draft_count = token_count // request_count
    share = HEADS // KV_HEADS
    rows_count = share * token_count
    tail = HEAD_DIM
    query = queries_ref[...].astype(jnp.float32)
    fresh = jnp.concatenate(
        [
            fresh_ref[...].astype(jnp.float32),
            jnp.zeros((tail - token_count, kv_width), jnp.float32),
        ],
        axis=0,
    ).astype(fresh_ref.dtype)
    pages = [table_ref[n, i] for n in range(request_count) for i in range(table_width)]

    def cache(first):
        rows = [pool_ref[page, :, first : first + HEAD_DIM] for page in pages]
        return jnp.concatenate(rows + [fresh[:, first : first + HEAD_DIM]], axis=0)

    token = lax.broadcasted_iota(jnp.int32, (rows_count, span), 0) % token_count
    lane = lax.broadcasted_iota(jnp.int32, (rows_count, span), 1)
    live = []
    for n in range(request_count):
        arrives = (table_ref[n, 0] == target_ref[0, 0]) | (table_ref[n, 0] == target_ref[1, 0])
        first = jnp.where(arrives, moved * page_tokens, 0)
        live.append((token // draft_count == n) & (lane >= first) & (lane < length_ref[n]))
    tail_token = lax.broadcasted_iota(jnp.int32, (rows_count, tail), 0) % token_count
    tail_lane = lax.broadcasted_iota(jnp.int32, (rows_count, tail), 1)
    live.append((tail_token // draft_count == tail_lane // draft_count) & (tail_lane <= tail_token))
    live = jnp.concatenate([jnp.where(mask, 0.0, neg_big) for mask in live], axis=1)
    key_width = KV_HEADS * HEAD_DIM
    for j in range(KV_HEADS):
        heads = range(j * share, (j + 1) * share)
        rows = jnp.concatenate([query[:, h * HEAD_DIM : (h + 1) * HEAD_DIM] for h in heads], axis=0)
        query_ref[j] = rows
        scores = lax.dot_general(
            rows.astype(jnp.bfloat16), cache(j * HEAD_DIM), (((1,), (1,)), ((), ())),
            preferred_element_type=jnp.float32,
        )
        scores = jnp.where(live < 0, neg_big, scores * HEAD_DIM ** (-0.5))
        highest = jnp.max(scores, axis=1, keepdims=True)
        weights = jnp.exp(scores - highest)
        max_ref[j] = jnp.broadcast_to(highest, max_ref.shape[1:])
        sum_ref[j] = jnp.broadcast_to(jnp.sum(weights, axis=1, keepdims=True), sum_ref.shape[1:])
        out_ref[j] = weighted_values(weights, cache(key_width + j * HEAD_DIM))

    moved_span = moved * page_tokens
    token = lax.broadcasted_iota(jnp.int32, (rows_count, 2 * moved_span), 0) % token_count
    lane = lax.broadcasted_iota(jnp.int32, (rows_count, 2 * moved_span), 1)
    seen = jnp.zeros((rows_count, 2 * moved_span), jnp.float32)
    odd = lax.rem(lax.axis_index("req"), 2)
    for block, side in enumerate((odd, 1 - odd)):
        position = lane - block * moved_span
        for n in range(request_count):
            bound = jnp.where(table_ref[n, 0] == target_ref[side, 0], length_ref[n], 0)
            inside = (position >= 0) & (position < moved_span) & (position < bound)
            seen = seen + jnp.where((token // draft_count == n) & inside, 1.0, 0.0)
    bias_ref[...] = jnp.where(seen > 0, 0.0, neg_big)


def local_attention(table, lengths, targets, queries, fresh_kv, pool_pages):
    token_count = queries.shape[0]
    moved = targets.shape[1]
    part = jax.ShapeDtypeStruct((KV_HEADS, HEADS // KV_HEADS * token_count, HEAD_DIM), jnp.float32)
    bias = jax.ShapeDtypeStruct((part.shape[1], 2 * moved * pool_pages.shape[1]), jnp.float32)
    return pl.pallas_call(
        local_attention_kernel,
        out_shape=(part, part, part, part, bias),
        in_specs=[pl.BlockSpec(memory_space=pltpu.SMEM)] * 3 + [pl.BlockSpec(memory_space=pltpu.VMEM)] * 3,
        out_specs=(pl.BlockSpec(memory_space=pltpu.VMEM),) * 5,
        compiler_params=pltpu.CompilerParams(vmem_limit_bytes=6 * 1024 * 1024),
        cost_estimate=pl.CostEstimate(flops=40 * 1024 * 1024, bytes_accessed=2 * 1024 * 1024, transcendentals=160 * 1024),
        name="local_attention",
    )(table, lengths, targets, queries, fresh_kv, pool_pages)


def arrived_attention_kernel(
    resid_ref, gain_ref, far_ref, near_ref, max_ref, sum_ref, out_ref, query_ref, bias_ref, residual_ref, normed_ref
):
    token_count, model_width = residual_ref.shape
    share = HEADS // KV_HEADS
    key_width = KV_HEADS * HEAD_DIM
    heads = range(KV_HEADS)

    def arrived(first):
        at = pl.ds(first, HEAD_DIM)
        return jnp.concatenate([far_ref[:, at], near_ref[:, at]], axis=0)

    scores = [
        lax.dot_general(
            query_ref[j].astype(jnp.bfloat16), arrived(j * HEAD_DIM), (((1,), (1,)), ((), ())),
            preferred_element_type=jnp.float32,
        )
        for j in heads
    ]
    hidden = bias_ref[...] < 0
    scores = [jnp.where(hidden, neg_big, part * HEAD_DIM ** (-0.5)) for part in scores]
    highest = [jnp.maximum(max_ref[j], jnp.max(scores[j], axis=1, keepdims=True)) for j in heads]
    weights = [jnp.exp(scores[j] - highest[j][:, :1]) for j in heads]
    scale = [jnp.exp(max_ref[j] - highest[j]) for j in heads]
    total = [sum_ref[j] * scale[j] + jnp.sum(weights[j], axis=1, keepdims=True) for j in heads]
    summed = [
        out_ref[j] * scale[j] + weighted_values(weights[j], arrived(key_width + j * HEAD_DIM)) for j in heads
    ]
    blocks = []
    for j in heads:
        attention = summed[j] / total[j]
        for h in range(share):
            first = (j * share + h) * HEAD_DIM
            resid = resid_ref[:, first : first + HEAD_DIM].astype(jnp.float32)
            blocks.append(resid + attention[h * token_count : (h + 1) * token_count])
    squares = blocks[0] * blocks[0]
    for block in blocks[1:]:
        squares = squares + block * block
    inv_rms = lax.rsqrt(jnp.sum(squares, axis=1, keepdims=True) / model_width + norm_eps)
    residual = jnp.concatenate(blocks, axis=1)
    residual_ref[...] = residual
    normed_ref[...] = (residual * inv_rms * gain_ref[...].astype(jnp.float32)[None, :]).astype(normed_ref.dtype)


def arrived_attention(resid_in, gain, far, near, parts):
    shape = resid_in.shape
    return pl.pallas_call(
        arrived_attention_kernel,
        out_shape=(jax.ShapeDtypeStruct(shape, jnp.float32), jax.ShapeDtypeStruct(shape, jnp.bfloat16)),
        in_specs=[pl.BlockSpec(memory_space=pltpu.VMEM)] * 9,
        out_specs=(pl.BlockSpec(memory_space=pltpu.VMEM),) * 2,
        compiler_params=pltpu.CompilerParams(vmem_limit_bytes=4 * 1024 * 1024),
        cost_estimate=pl.CostEstimate(flops=1024 * 1024 * 1024, bytes_accessed=2 * 1024 * 1024, transcendentals=60 * 1024),
        name="arrived_attention",
    )(resid_in, gain, far, near, *parts)


def pack_kernel(columns_ref, *refs):
    out_refs = refs[-EXP_DEV:]
    rows = jnp.concatenate([ref[...].astype(jnp.float32) for ref in refs[:-EXP_DEV]], axis=0)
    slots = jnp.dot(columns_ref[...], rows.astype(jnp.bfloat16), preferred_element_type=jnp.float32)
    for k, out_ref in enumerate(out_refs):
        out_ref[...] = slots[k * CAP : (k + 1) * CAP].astype(out_ref.dtype)


def pack(columns, parts):
    slots = jax.ShapeDtypeStruct((CAP, parts[0].shape[1]), parts[0].dtype)
    return pl.pallas_call(
        pack_kernel,
        out_shape=(slots,) * EXP_DEV,
        in_specs=[pl.BlockSpec(memory_space=pltpu.VMEM)] * (1 + len(parts)),
        out_specs=(pl.BlockSpec(memory_space=pltpu.VMEM),) * EXP_DEV,
        compiler_params=pltpu.CompilerParams(vmem_limit_bytes=8 * 1024 * 1024),
        cost_estimate=pl.CostEstimate(
            flops=8 * 1024 * 1024 * 1024, bytes_accessed=2 * 1024 * 1024, transcendentals=0
        ),
        name="pack",
    )(columns.reshape(EXP_DEV * CAP, -1), *parts)


def expert_kernel(rows_ref, inner_ref, outer_ref, own_ref, others_ref):
    rows = rows_ref[...]
    own = own_ref.shape[0]
    tile = min(2 * HEAD_DIM, inner_ref.shape[1])
    parts = []
    for c in range(0, inner_ref.shape[1], tile):
        hidden = jnp.dot(rows, inner_ref[:, c : c + tile], preferred_element_type=jnp.float32)
        parts.append((hidden / (1.0 + jnp.exp(-hidden))).astype(rows.dtype))
    activated = jnp.concatenate(parts, axis=1)
    tile = 2 * HEAD_DIM
    for c in range(0, own_ref.shape[1], tile):
        out = jnp.dot(activated, outer_ref[:, c : c + tile], preferred_element_type=jnp.float32)
        own_ref[:, c : c + tile] = out[:own]
        others_ref[:, c : c + tile] = out[own:].astype(others_ref.dtype)


def expert(rows, inner, outer, own):
    return pl.pallas_call(
        expert_kernel,
        out_shape=(
            jax.ShapeDtypeStruct((own, outer.shape[1]), jnp.float32),
            jax.ShapeDtypeStruct((rows.shape[0] - own, outer.shape[1]), rows.dtype),
        ),
        in_specs=[pl.BlockSpec(memory_space=pltpu.VMEM)] * 3,
        out_specs=(pl.BlockSpec(memory_space=pltpu.VMEM),) * 2,
        compiler_params=pltpu.CompilerParams(vmem_limit_bytes=32 * 1024 * 1024),
        cost_estimate=pl.CostEstimate(
            flops=2 * rows.shape[0] * (inner.size + outer.size),
            bytes_accessed=(inner.size + outer.size) * inner.dtype.itemsize,
            transcendentals=rows.shape[0] * inner.shape[1],
        ),
        name="expert",
    )(rows, inner, outer)


def combine_kernel(gate_ref, residual_ref, *refs):
    block_refs, out_refs = refs[:EXP_DEV], refs[EXP_DEV:]
    rows = jnp.concatenate([ref[...].astype(jnp.float32) for ref in block_refs], axis=0).astype(jnp.bfloat16)
    gates = jnp.concatenate([gate_ref[k] for k in range(EXP_DEV)], axis=0)
    high = gates.astype(jnp.bfloat16)
    low = (gates - high.astype(jnp.float32)).astype(jnp.bfloat16)
    mix = lax.dot_general(
        jnp.concatenate([high.astype(jnp.float32), low.astype(jnp.float32)], axis=1).astype(jnp.bfloat16), rows,
        (((0,), (0,)), ((), ())), preferred_element_type=jnp.float32,
    )
    half = gates.shape[1]
    mix = mix[:half] + mix[half:]
    count = out_refs[0].shape[0]
    out_refs[0][...] = residual_ref[...] + mix[:count]
    for k, out_ref in enumerate(out_refs[1:]):
        out_ref[...] = mix[(k + 1) * count : (k + 2) * count].astype(out_ref.dtype)


def combine(gate_columns, residual, blocks, partners):
    sent = jax.ShapeDtypeStruct(residual.shape, jnp.bfloat16)
    return pl.pallas_call(
        combine_kernel,
        out_shape=(jax.ShapeDtypeStruct(residual.shape, jnp.float32),) + (sent,) * partners,
        in_specs=[pl.BlockSpec(memory_space=pltpu.VMEM)] * (2 + len(blocks)),
        out_specs=(pl.BlockSpec(memory_space=pltpu.VMEM),) * (1 + partners),
        compiler_params=pltpu.CompilerParams(vmem_limit_bytes=12 * 1024 * 1024),
        cost_estimate=pl.CostEstimate(
            flops=4 * gate_columns.size * residual.shape[1], bytes_accessed=4 * 1024 * 1024, transcendentals=0
        ),
        name="combine",
    )(gate_columns, residual, *blocks)


def body(
    resid_in,
    queries,
    fresh_kv,
    kv_pool,
    block_table,
    lengths,
    mig_source,
    mig_target,
    expert_ids,
    gate_values,
    norm_gain,
    w_in,
    w_out,
):
    token_count = resid_in.shape[0]
    model_width = resid_in.shape[1]
    exp_count = lax.axis_size("exp")
    group_size = lax.axis_size("req") // EXP_DEV
    plane_orders = PLANE_ORDERS
    member = lax.axis_index("req") % group_size
    group_steps = partner_steps(group_size)
    falling = list(range(exp_count - 1, 0, -1))
    exp_orders = (falling, falling[1::-1] + falling[2:])

    pool_pages = kv_pool[0, 0]
    targets = mig_target[0, 0]
    far, near = send_pages(pool_pages, mig_source[0, 0], opening())
    moved_shape = (far.shape[0] * far.shape[1], far.shape[2])
    far = swap_ring(far.reshape(moved_shape), 1)
    near = swap_ring(near.reshape(moved_shape), 0)

    parts = local_attention(block_table, lengths, targets, queries, fresh_kv, pool_pages)
    residual, normed = arrived_attention(resid_in, norm_gain, far, near, parts)
    normed, expert_ids, gate_values = lax.optimization_barrier((normed, expert_ids, gate_values))

    exp_order = partner_of(lax.axis_index("exp"), exp_orders, member)
    plane_order = partner_of(lax.axis_index("req") // group_size, plane_orders, member)
    ids = expert_ids.reshape(exp_count, token_count, -1)[exp_order].reshape(expert_ids.shape)
    gates = gate_values.reshape(exp_count, token_count, -1)[exp_order].reshape(gate_values.shape)
    local_ids = lax.axis_index("exp") * EXP_DEV + plane_order
    matches = ids[None, :, :] == local_ids[:, None, None]
    is_named = jnp.any(matches, axis=2)
    gate_local = jnp.sum(jnp.where(matches, gates[None, :, :], 0.0), axis=2)
    slot_index = jnp.cumsum(is_named.astype(jnp.int32), axis=1) - 1
    placement = is_named[:, None, :] & (slot_index[:, None, :] == jnp.arange(CAP)[None, :, None])
    columns = placement.astype(jnp.bfloat16)
    gate_columns = jnp.where(placement, gate_local[:, None, :], 0.0)

    packed = pack(columns, [normed] + [swap_exp(normed, k, exp_orders, group_size) for k in range(exp_count - 1)])
    pieces = [packed[0]] + [
        swap_plane(packed[k + 1], k, plane_orders, group_size) for k in range(EXP_DEV - 1)
    ]
    inbound = jnp.concatenate(
        pieces + [swap_group(piece, step, group_size) for step in group_steps for piece in pieces], axis=0
    )

    share = EXP_DEV * CAP
    summed, others = expert(inbound, w_in[0, 0], w_out[0, 0], share)
    arrived = [
        swap_group(others[k * share : (k + 1) * share], step, group_size) for k, step in enumerate(group_steps)
    ]
    for part in arrived:
        summed = summed + part.astype(jnp.float32)
    summed = summed.astype(jnp.bfloat16)

    returned = [summed[:CAP]] + [
        swap_plane(summed[(k + 1) * CAP : (k + 2) * CAP], k, plane_orders, group_size) for k in range(EXP_DEV - 1)
    ]
    result, *blocks = combine(gate_columns, residual, returned, exp_count - 1)
    for k, block in enumerate(blocks):
        result = result + swap_exp(block, k, exp_orders, group_size).astype(jnp.float32)
    return result.astype(jnp.bfloat16)


def solution(mesh):
    placed = (
        P(("req", "exp"), None),
        P(("req", "exp"), None),
        P(("req", "exp"), None),
        P("req", "exp", None, None, None),
        P(("req", "exp"), None),
        P(("req", "exp")),
        P("req", "exp", None, None),
        P("req", "exp", None, None),
        P("req", None),
        P("req", None),
        P(),
        P("exp", "req", None, None),
        P("exp", "req", None, None),
    )
    return jax.shard_map(
        body, mesh=mesh, in_specs=placed, out_specs=P(("req", "exp"), None), check_vma=False
    )
```

```python
import jax
import jax.numpy as jnp
from jax import lax
from jax.experimental import pallas as pl
from jax.experimental.pallas import tpu as pltpu
from jax.sharding import PartitionSpec as P

HEADS = 28
KV_HEADS = 4
HEAD_DIM = 128
EXP_DEV = 4
CAP = 24
PLANE_ORDERS = ((2, 3, 1), (1, 3, 2))
RETURN_ORDER = (0, 3, 2, 1)


neg_big = -1e30
norm_eps = 1e-06


def partner_steps(count):
    if count & (count - 1):
        raise ValueError("axis size")
    return [[i ^ k for i in range(count)] for k in range(1, count)]


def partner_of(index, orders, member):
    return index ^ jnp.array([[0] + list(order) for order in orders], dtype=jnp.int32)[member % len(orders)]


def swap_ring(block, offset):
    count = lax.axis_size("req")
    if count % 2:
        raise ValueError("axis size")
    pairs = []
    for i in range(offset, count, 2):
        pairs += [(i, (i + 1) % count), ((i + 1) % count, i)]
    return lax.ppermute(block, "req", pairs)


def swap_plane(block, k, orders, group_size):
    pairs = [
        (q * group_size + g, (q ^ orders[g % len(orders)][k]) * group_size + g)
        for q in range(EXP_DEV)
        for g in range(group_size)
    ]
    return lax.ppermute(block, "req", pairs)


def swap_group(block, step, group_size):
    pairs = [(q * group_size + g, q * group_size + p) for q in range(EXP_DEV) for g, p in enumerate(step)]
    return lax.ppermute(block, "req", pairs)


def swap_exp(block, k, orders, group_size):
    count = lax.axis_size("exp")
    pairs = [
        (r * count + e, r * count + (e ^ orders[r % group_size % len(orders)][k]))
        for r in range(lax.axis_size("req"))
        for e in range(count)
    ]
    return lax.ppermute(block, ("req", "exp"), pairs)


def opening_kernel(out_ref):
    out_ref[...] = jnp.zeros_like(out_ref)


def opening():
    return pl.pallas_call(
        opening_kernel,
        out_shape=jax.ShapeDtypeStruct((8, HEAD_DIM), jnp.float32),
        out_specs=pl.BlockSpec(memory_space=pltpu.VMEM),
        compiler_params=pltpu.CompilerParams(vmem_limit_bytes=1024 * 1024),
        cost_estimate=pl.CostEstimate(flops=4 * 1024 * 1024 * 1024, bytes_accessed=4096, transcendentals=0),
        name="opening",
    )()


def send_pages_kernel(source_ref, pool_ref, after_ref, far_ref, near_ref):
    odd = lax.rem(lax.axis_index("req"), 2)
    for side, out_ref in ((1 - odd, far_ref), (odd, near_ref)):
        for i in range(out_ref.shape[0]):
            out_ref[i] = pool_ref[source_ref[side, i]]


def send_pages(pool_pages, sources, after):
    pages = jax.ShapeDtypeStruct((sources.shape[1],) + pool_pages.shape[1:], pool_pages.dtype)
    return pl.pallas_call(
        send_pages_kernel,
        out_shape=(pages, pages),
        in_specs=[pl.BlockSpec(memory_space=pltpu.SMEM)] + [pl.BlockSpec(memory_space=pltpu.VMEM)] * 2,
        out_specs=(pl.BlockSpec(memory_space=pltpu.VMEM),) * 2,
        compiler_params=pltpu.CompilerParams(vmem_limit_bytes=4 * 1024 * 1024),
        cost_estimate=pl.CostEstimate(
            flops=4 * 1024 * 1024 * 1024, bytes_accessed=pool_pages.size * pool_pages.dtype.itemsize, transcendentals=0
        ),
        name="send_pages",
    )(sources, pool_pages, after)


def weighted_values(weights, values):
    high = weights.astype(jnp.bfloat16)
    low = (weights - high.astype(jnp.float32)).astype(jnp.bfloat16)
    both = jnp.dot(
        jnp.concatenate([high, low], axis=0), values, preferred_element_type=jnp.float32
    )
    return both[: weights.shape[0]] + both[weights.shape[0] :]


def local_attention_kernel(
    table_ref, length_ref, target_ref, queries_ref, fresh_ref, pool_ref, max_ref, sum_ref, out_ref, query_ref, bias_ref
):
    request_count, table_width = table_ref.shape
    token_count, kv_width = fresh_ref.shape
    moved = target_ref.shape[1]
    page_tokens = pool_ref.shape[1]
    span = table_width * page_tokens
    draft_count = token_count // request_count
    share = HEADS // KV_HEADS
    rows_count = share * token_count
    tail = HEAD_DIM
    query = queries_ref[...].astype(jnp.float32)
    fresh = jnp.concatenate(
        [
            fresh_ref[...].astype(jnp.float32),
            jnp.zeros((tail - token_count, kv_width), jnp.float32),
        ],
        axis=0,
    ).astype(fresh_ref.dtype)
    pages = [table_ref[n, i] for n in range(request_count) for i in range(table_width)]

    def cache(first):
        rows = [pool_ref[page, :, first : first + HEAD_DIM] for page in pages]
        return jnp.concatenate(rows + [fresh[:, first : first + HEAD_DIM]], axis=0)

    token = lax.broadcasted_iota(jnp.int32, (rows_count, span), 0) % token_count
    lane = lax.broadcasted_iota(jnp.int32, (rows_count, span), 1)
    live = []
    for n in range(request_count):
        arrives = (table_ref[n, 0] == target_ref[0, 0]) | (table_ref[n, 0] == target_ref[1, 0])
        first = jnp.where(arrives, moved * page_tokens, 0)
        live.append((token // draft_count == n) & (lane >= first) & (lane < length_ref[n]))
    tail_token = lax.broadcasted_iota(jnp.int32, (rows_count, tail), 0) % token_count
    tail_lane = lax.broadcasted_iota(jnp.int32, (rows_count, tail), 1)
    live.append((tail_token // draft_count == tail_lane // draft_count) & (tail_lane <= tail_token))
    live = jnp.concatenate([jnp.where(mask, 0.0, neg_big) for mask in live], axis=1)
    key_width = KV_HEADS * HEAD_DIM
    for j in range(KV_HEADS):
        heads = range(j * share, (j + 1) * share)
        rows = jnp.concatenate([query[:, h * HEAD_DIM : (h + 1) * HEAD_DIM] for h in heads], axis=0)
        query_ref[j] = rows
        scores = lax.dot_general(
            rows.astype(jnp.bfloat16), cache(j * HEAD_DIM), (((1,), (1,)), ((), ())),
            preferred_element_type=jnp.float32,
        )
        scores = jnp.where(live < 0, neg_big, scores * HEAD_DIM ** (-0.5))
        highest = jnp.max(scores, axis=1, keepdims=True)
        weights = jnp.exp(scores - highest)
        max_ref[j] = jnp.broadcast_to(highest, max_ref.shape[1:])
        sum_ref[j] = jnp.broadcast_to(jnp.sum(weights, axis=1, keepdims=True), sum_ref.shape[1:])
        out_ref[j] = weighted_values(weights, cache(key_width + j * HEAD_DIM))

    moved_span = moved * page_tokens
    token = lax.broadcasted_iota(jnp.int32, (rows_count, 2 * moved_span), 0) % token_count
    lane = lax.broadcasted_iota(jnp.int32, (rows_count, 2 * moved_span), 1)
    seen = jnp.zeros((rows_count, 2 * moved_span), jnp.float32)
    odd = lax.rem(lax.axis_index("req"), 2)
    for block, side in enumerate((odd, 1 - odd)):
        position = lane - block * moved_span
        for n in range(request_count):
            bound = jnp.where(table_ref[n, 0] == target_ref[side, 0], length_ref[n], 0)
            inside = (position >= 0) & (position < moved_span) & (position < bound)
            seen = seen + jnp.where((token // draft_count == n) & inside, 1.0, 0.0)
    bias_ref[...] = jnp.where(seen > 0, 0.0, neg_big)


def local_attention(table, lengths, targets, queries, fresh_kv, pool_pages):
    token_count = queries.shape[0]
    moved = targets.shape[1]
    part = jax.ShapeDtypeStruct((KV_HEADS, HEADS // KV_HEADS * token_count, HEAD_DIM), jnp.float32)
    bias = jax.ShapeDtypeStruct((part.shape[1], 2 * moved * pool_pages.shape[1]), jnp.float32)
    return pl.pallas_call(
        local_attention_kernel,
        out_shape=(part, part, part, part, bias),
        in_specs=[pl.BlockSpec(memory_space=pltpu.SMEM)] * 3 + [pl.BlockSpec(memory_space=pltpu.VMEM)] * 3,
        out_specs=(pl.BlockSpec(memory_space=pltpu.VMEM),) * 5,
        compiler_params=pltpu.CompilerParams(vmem_limit_bytes=6 * 1024 * 1024),
        cost_estimate=pl.CostEstimate(flops=40 * 1024 * 1024, bytes_accessed=2 * 1024 * 1024, transcendentals=160 * 1024),
        name="local_attention",
    )(table, lengths, targets, queries, fresh_kv, pool_pages)


def arrived_attention_kernel(
    resid_ref, gain_ref, far_ref, near_ref, max_ref, sum_ref, out_ref, query_ref, bias_ref, residual_ref, normed_ref
):
    token_count, model_width = residual_ref.shape
    share = HEADS // KV_HEADS
    key_width = KV_HEADS * HEAD_DIM
    heads = range(KV_HEADS)

    def arrived(first):
        at = pl.ds(first, HEAD_DIM)
        return jnp.concatenate([far_ref[:, at], near_ref[:, at]], axis=0)

    scores = [
        lax.dot_general(
            query_ref[j].astype(jnp.bfloat16), arrived(j * HEAD_DIM), (((1,), (1,)), ((), ())),
            preferred_element_type=jnp.float32,
        )
        for j in heads
    ]
    hidden = bias_ref[...] < 0
    scores = [jnp.where(hidden, neg_big, part * HEAD_DIM ** (-0.5)) for part in scores]
    highest = [jnp.maximum(max_ref[j], jnp.max(scores[j], axis=1, keepdims=True)) for j in heads]
    weights = [jnp.exp(scores[j] - highest[j][:, :1]) for j in heads]
    scale = [jnp.exp(max_ref[j] - highest[j]) for j in heads]
    total = [sum_ref[j] * scale[j] + jnp.sum(weights[j], axis=1, keepdims=True) for j in heads]
    summed = [
        out_ref[j] * scale[j] + weighted_values(weights[j], arrived(key_width + j * HEAD_DIM)) for j in heads
    ]
    blocks = []
    for j in heads:
        attention = summed[j] / total[j]
        for h in range(share):
            first = (j * share + h) * HEAD_DIM
            resid = resid_ref[:, first : first + HEAD_DIM].astype(jnp.float32)
            blocks.append(resid + attention[h * token_count : (h + 1) * token_count])
    squares = blocks[0] * blocks[0]
    for block in blocks[1:]:
        squares = squares + block * block
    inv_rms = lax.rsqrt(jnp.sum(squares, axis=1, keepdims=True) / model_width + norm_eps)
    residual = jnp.concatenate(blocks, axis=1)
    residual_ref[...] = residual
    normed_ref[...] = (residual * inv_rms * gain_ref[...].astype(jnp.float32)[None, :]).astype(normed_ref.dtype)


def arrived_attention(resid_in, gain, far, near, parts):
    shape = resid_in.shape
    return pl.pallas_call(
        arrived_attention_kernel,
        out_shape=(jax.ShapeDtypeStruct(shape, jnp.float32), jax.ShapeDtypeStruct(shape, jnp.bfloat16)),
        in_specs=[pl.BlockSpec(memory_space=pltpu.VMEM)] * 9,
        out_specs=(pl.BlockSpec(memory_space=pltpu.VMEM),) * 2,
        compiler_params=pltpu.CompilerParams(vmem_limit_bytes=4 * 1024 * 1024),
        cost_estimate=pl.CostEstimate(flops=1024 * 1024 * 1024, bytes_accessed=2 * 1024 * 1024, transcendentals=60 * 1024),
        name="arrived_attention",
    )(resid_in, gain, far, near, *parts)


def pack_kernel(columns_ref, *refs):
    out_refs = refs[-EXP_DEV:]
    rows = jnp.concatenate([ref[...].astype(jnp.float32) for ref in refs[:-EXP_DEV]], axis=0)
    slots = jnp.dot(columns_ref[...], rows.astype(jnp.bfloat16), preferred_element_type=jnp.float32)
    for k, out_ref in enumerate(out_refs):
        out_ref[...] = slots[k * CAP : (k + 1) * CAP].astype(out_ref.dtype)


def pack(columns, parts):
    slots = jax.ShapeDtypeStruct((CAP, parts[0].shape[1]), parts[0].dtype)
    return pl.pallas_call(
        pack_kernel,
        out_shape=(slots,) * EXP_DEV,
        in_specs=[pl.BlockSpec(memory_space=pltpu.VMEM)] * (1 + len(parts)),
        out_specs=(pl.BlockSpec(memory_space=pltpu.VMEM),) * EXP_DEV,
        compiler_params=pltpu.CompilerParams(vmem_limit_bytes=8 * 1024 * 1024),
        cost_estimate=pl.CostEstimate(
            flops=8 * 1024 * 1024 * 1024, bytes_accessed=2 * 1024 * 1024, transcendentals=0
        ),
        name="pack",
    )(columns.reshape(EXP_DEV * CAP, -1), *parts)


def expert_kernel(rows_ref, inner_ref, outer_ref, *out_refs):
    rows = rows_ref[...]
    tile = min(2 * HEAD_DIM, inner_ref.shape[1])
    parts = []
    for c in range(0, inner_ref.shape[1], tile):
        hidden = jnp.dot(rows, inner_ref[:, c : c + tile], preferred_element_type=jnp.float32)
        parts.append((hidden / (1.0 + jnp.exp(-hidden))).astype(rows.dtype))
    activated = jnp.concatenate(parts, axis=1)
    tile = 2 * HEAD_DIM
    for c in range(0, outer_ref.shape[1], tile):
        out = jnp.dot(activated, outer_ref[:, c : c + tile], preferred_element_type=jnp.float32)
        for k, out_ref in enumerate(out_refs):
            out_ref[:, c : c + tile] = out[k * CAP : (k + 1) * CAP].astype(out_ref.dtype)


def expert(rows, inner, outer):
    width = outer.shape[1]
    others = rows.shape[0] // CAP - EXP_DEV
    out_shape = (jax.ShapeDtypeStruct((CAP, width), jnp.float32),) * EXP_DEV
    out_shape += (jax.ShapeDtypeStruct((CAP, width), rows.dtype),) * others
    return pl.pallas_call(
        expert_kernel,
        out_shape=out_shape,
        in_specs=[pl.BlockSpec(memory_space=pltpu.VMEM)] * 3,
        out_specs=(pl.BlockSpec(memory_space=pltpu.VMEM),) * len(out_shape),
        compiler_params=pltpu.CompilerParams(vmem_limit_bytes=32 * 1024 * 1024),
        cost_estimate=pl.CostEstimate(
            flops=2 * rows.shape[0] * (inner.size + outer.size),
            bytes_accessed=(inner.size + outer.size) * inner.dtype.itemsize,
            transcendentals=rows.shape[0] * inner.shape[1],
        ),
        name="expert",
    )(rows, inner, outer)


def combine_kernel(gate_ref, residual_ref, *refs):
    block_refs, out_refs = refs[:EXP_DEV], refs[EXP_DEV:]
    rows = jnp.concatenate([ref[...].astype(jnp.float32) for ref in block_refs], axis=0).astype(jnp.bfloat16)
    gates = jnp.concatenate([gate_ref[k] for k in RETURN_ORDER], axis=0)
    high = gates.astype(jnp.bfloat16)
    low = (gates - high.astype(jnp.float32)).astype(jnp.bfloat16)
    mix = lax.dot_general(
        jnp.concatenate([high.astype(jnp.float32), low.astype(jnp.float32)], axis=1).astype(jnp.bfloat16), rows,
        (((0,), (0,)), ((), ())), preferred_element_type=jnp.float32,
    )
    half = gates.shape[1]
    mix = mix[:half] + mix[half:]
    count = out_refs[0].shape[0]
    out_refs[0][...] = residual_ref[...] + mix[:count]
    for k, out_ref in enumerate(out_refs[1:]):
        out_ref[...] = mix[(k + 1) * count : (k + 2) * count].astype(out_ref.dtype)


def combine(gate_columns, residual, blocks, partners):
    sent = jax.ShapeDtypeStruct(residual.shape, jnp.bfloat16)
    return pl.pallas_call(
        combine_kernel,
        out_shape=(jax.ShapeDtypeStruct(residual.shape, jnp.float32),) + (sent,) * partners,
        in_specs=[pl.BlockSpec(memory_space=pltpu.VMEM)] * (2 + len(blocks)),
        out_specs=(pl.BlockSpec(memory_space=pltpu.VMEM),) * (1 + partners),
        compiler_params=pltpu.CompilerParams(vmem_limit_bytes=12 * 1024 * 1024),
        cost_estimate=pl.CostEstimate(
            flops=4 * gate_columns.size * residual.shape[1], bytes_accessed=4 * 1024 * 1024, transcendentals=0
        ),
        name="combine",
    )(gate_columns, residual, *[blocks[k] for k in RETURN_ORDER])


def body(
    resid_in,
    queries,
    fresh_kv,
    kv_pool,
    block_table,
    lengths,
    mig_source,
    mig_target,
    expert_ids,
    gate_values,
    norm_gain,
    w_in,
    w_out,
):
    token_count = resid_in.shape[0]
    model_width = resid_in.shape[1]
    exp_count = lax.axis_size("exp")
    group_size = lax.axis_size("req") // EXP_DEV
    plane_orders = PLANE_ORDERS
    member = lax.axis_index("req") % group_size
    group_steps = partner_steps(group_size)
    falling = list(range(exp_count - 1, 0, -1))
    exp_orders = (falling, falling[1::-1] + falling[2:])

    pool_pages = kv_pool[0, 0]
    targets = mig_target[0, 0]
    far, near = send_pages(pool_pages, mig_source[0, 0], opening())
    moved_shape = (far.shape[0] * far.shape[1], far.shape[2])
    far = swap_ring(far.reshape(moved_shape), 1)
    near = swap_ring(near.reshape(moved_shape), 0)

    parts = local_attention(block_table, lengths, targets, queries, fresh_kv, pool_pages)
    residual, normed = arrived_attention(resid_in, norm_gain, far, near, parts)
    normed, expert_ids, gate_values = lax.optimization_barrier((normed, expert_ids, gate_values))

    exp_order = partner_of(lax.axis_index("exp"), exp_orders, member)
    plane_order = partner_of(lax.axis_index("req") // group_size, plane_orders, member)
    ids = expert_ids.reshape(exp_count, token_count, -1)[exp_order].reshape(expert_ids.shape)
    gates = gate_values.reshape(exp_count, token_count, -1)[exp_order].reshape(gate_values.shape)
    local_ids = lax.axis_index("exp") * EXP_DEV + plane_order
    matches = ids[None, :, :] == local_ids[:, None, None]
    is_named = jnp.any(matches, axis=2)
    gate_local = jnp.sum(jnp.where(matches, gates[None, :, :], 0.0), axis=2)
    slot_index = jnp.cumsum(is_named.astype(jnp.int32), axis=1) - 1
    placement = is_named[:, None, :] & (slot_index[:, None, :] == jnp.arange(CAP)[None, :, None])
    columns = placement.astype(jnp.bfloat16)
    gate_columns = jnp.where(placement, gate_local[:, None, :], 0.0)

    packed = pack(columns, [normed] + [swap_exp(normed, k, exp_orders, group_size) for k in range(exp_count - 1)])
    pieces = [packed[0]] + [
        swap_plane(packed[k + 1], k, plane_orders, group_size) for k in range(EXP_DEV - 1)
    ]
    inbound = jnp.concatenate(
        pieces + [swap_group(piece, step, group_size) for step in group_steps for piece in pieces], axis=0
    )

    slots = expert(inbound, w_in[0, 0], w_out[0, 0])
    summed = []
    for j in range(EXP_DEV):
        total = slots[j]
        for k, step in enumerate(group_steps):
            total = total + swap_group(slots[(k + 1) * EXP_DEV + j], step, group_size).astype(jnp.float32)
        summed.append(total.astype(jnp.bfloat16))

    returned = [summed[0]] + [
        swap_plane(summed[k + 1], k, plane_orders, group_size) for k in range(EXP_DEV - 1)
    ]
    result, *blocks = combine(gate_columns, residual, returned, exp_count - 1)
    for k in [0] + list(range(exp_count - 2, 0, -1)):
        result = result + swap_exp(blocks[k], k, exp_orders, group_size).astype(jnp.float32)
    return result.astype(jnp.bfloat16)


def solution(mesh):
    placed = (
        P(("req", "exp"), None),
        P(("req", "exp"), None),
        P(("req", "exp"), None),
        P("req", "exp", None, None, None),
        P(("req", "exp"), None),
        P(("req", "exp")),
        P("req", "exp", None, None),
        P("req", "exp", None, None),
        P("req", None),
        P("req", None),
        P(),
        P("exp", "req", None, None),
        P("exp", "req", None, None),
    )
    return jax.shard_map(
        body, mesh=mesh, in_specs=placed, out_specs=P(("req", "exp"), None), check_vma=False
    )
```

```python
import functools

import jax
import jax.numpy as jnp
from jax import lax
from jax.experimental import pallas as pl
from jax.experimental.pallas import tpu as pltpu
from jax.sharding import PartitionSpec as P

HEADS = 28
KV_HEADS = 4
HEAD_DIM = 128
EXP_DEV = 4
CAP = 24
PLANE_ORDERS = ((2, 3, 1), (1, 3, 2))
RETURN_ORDER = (0, 3, 2, 1)


neg_big = -1e30
norm_eps = 1e-06


def partner_steps(count):
    if count & (count - 1):
        raise ValueError("axis size")
    return [[i ^ k for i in range(count)] for k in range(1, count)]


def partner_of(index, orders, member):
    return index ^ jnp.array([[0] + list(order) for order in orders], dtype=jnp.int32)[member % len(orders)]


def swap_ring(block, offset):
    count = lax.axis_size("req")
    if count % 2:
        raise ValueError("axis size")
    pairs = []
    for i in range(offset, count, 2):
        pairs += [(i, (i + 1) % count), ((i + 1) % count, i)]
    return lax.ppermute(block, "req", pairs)


def swap_plane(block, k, orders, group_size):
    pairs = [
        (q * group_size + g, (q ^ orders[g % len(orders)][k]) * group_size + g)
        for q in range(EXP_DEV)
        for g in range(group_size)
    ]
    return lax.ppermute(block, "req", pairs)


def swap_group(block, step, group_size):
    pairs = [(q * group_size + g, q * group_size + p) for q in range(EXP_DEV) for g, p in enumerate(step)]
    return lax.ppermute(block, "req", pairs)


def swap_exp(block, k, orders, group_size):
    count = lax.axis_size("exp")
    pairs = [
        (r * count + e, r * count + (e ^ orders[r % group_size % len(orders)][k]))
        for r in range(lax.axis_size("req"))
        for e in range(count)
    ]
    return lax.ppermute(block, ("req", "exp"), pairs)


def opening_kernel(out_ref):
    out_ref[...] = jnp.zeros_like(out_ref)


def opening():
    return pl.pallas_call(
        opening_kernel,
        out_shape=jax.ShapeDtypeStruct((8, HEAD_DIM), jnp.float32),
        out_specs=pl.BlockSpec(memory_space=pltpu.VMEM),
        compiler_params=pltpu.CompilerParams(vmem_limit_bytes=1024 * 1024),
        cost_estimate=pl.CostEstimate(flops=4 * 1024 * 1024 * 1024, bytes_accessed=4096, transcendentals=0),
        name="opening",
    )()


def send_pages_kernel(source_ref, pool_ref, after_ref, out_ref, *, far):
    odd = lax.rem(lax.axis_index("req"), 2)
    side = 1 - odd if far else odd
    for i in range(out_ref.shape[0]):
        out_ref[i] = pool_ref[source_ref[side, i]]


def send_pages(pool_pages, sources, after, far):
    pages = jax.ShapeDtypeStruct((sources.shape[1],) + pool_pages.shape[1:], pool_pages.dtype)
    return pl.pallas_call(
        functools.partial(send_pages_kernel, far=far),
        out_shape=pages,
        in_specs=[pl.BlockSpec(memory_space=pltpu.SMEM)] + [pl.BlockSpec(memory_space=pltpu.VMEM)] * 2,
        out_specs=pl.BlockSpec(memory_space=pltpu.VMEM),
        compiler_params=pltpu.CompilerParams(vmem_limit_bytes=4 * 1024 * 1024),
        cost_estimate=pl.CostEstimate(
            flops=4 * 1024 * 1024 * 1024, bytes_accessed=pool_pages.size * pool_pages.dtype.itemsize, transcendentals=0
        ),
        name="send_pages",
    )(sources, pool_pages, after)


def weighted_values(weights, values):
    high = weights.astype(jnp.bfloat16)
    low = (weights - high.astype(jnp.float32)).astype(jnp.bfloat16)
    both = jnp.dot(
        jnp.concatenate([high, low], axis=0), values, preferred_element_type=jnp.float32
    )
    return both[: weights.shape[0]] + both[weights.shape[0] :]


def local_attention_kernel(
    table_ref, length_ref, target_ref, queries_ref, fresh_ref, pool_ref, max_ref, sum_ref, out_ref, query_ref, bias_ref
):
    request_count, table_width = table_ref.shape
    token_count, kv_width = fresh_ref.shape
    moved = target_ref.shape[1]
    page_tokens = pool_ref.shape[1]
    span = table_width * page_tokens
    draft_count = token_count // request_count
    share = HEADS // KV_HEADS
    rows_count = share * token_count
    tail = HEAD_DIM
    query = queries_ref[...].astype(jnp.float32)
    fresh = jnp.concatenate(
        [
            fresh_ref[...].astype(jnp.float32),
            jnp.zeros((tail - token_count, kv_width), jnp.float32),
        ],
        axis=0,
    ).astype(fresh_ref.dtype)
    pages = [table_ref[n, i] for n in range(request_count) for i in range(table_width)]

    def cache(first):
        rows = [pool_ref[page, :, first : first + HEAD_DIM] for page in pages]
        return jnp.concatenate(rows + [fresh[:, first : first + HEAD_DIM]], axis=0)

    token = lax.broadcasted_iota(jnp.int32, (rows_count, span), 0) % token_count
    lane = lax.broadcasted_iota(jnp.int32, (rows_count, span), 1)
    live = []
    for n in range(request_count):
        arrives = (table_ref[n, 0] == target_ref[0, 0]) | (table_ref[n, 0] == target_ref[1, 0])
        first = jnp.where(arrives, moved * page_tokens, 0)
        live.append((token // draft_count == n) & (lane >= first) & (lane < length_ref[n]))
    tail_token = lax.broadcasted_iota(jnp.int32, (rows_count, tail), 0) % token_count
    tail_lane = lax.broadcasted_iota(jnp.int32, (rows_count, tail), 1)
    live.append((tail_token // draft_count == tail_lane // draft_count) & (tail_lane <= tail_token))
    live = jnp.concatenate([jnp.where(mask, 0.0, neg_big) for mask in live], axis=1)
    key_width = KV_HEADS * HEAD_DIM
    for j in range(KV_HEADS):
        heads = range(j * share, (j + 1) * share)
        rows = jnp.concatenate([query[:, h * HEAD_DIM : (h + 1) * HEAD_DIM] for h in heads], axis=0)
        query_ref[j] = rows
        scores = lax.dot_general(
            rows.astype(jnp.bfloat16), cache(j * HEAD_DIM), (((1,), (1,)), ((), ())),
            preferred_element_type=jnp.float32,
        )
        scores = jnp.where(live < 0, neg_big, scores * HEAD_DIM ** (-0.5))
        highest = jnp.max(scores, axis=1, keepdims=True)
        weights = jnp.exp(scores - highest)
        max_ref[j] = jnp.broadcast_to(highest, max_ref.shape[1:])
        sum_ref[j] = jnp.broadcast_to(jnp.sum(weights, axis=1, keepdims=True), sum_ref.shape[1:])
        out_ref[j] = weighted_values(weights, cache(key_width + j * HEAD_DIM))

    moved_span = moved * page_tokens
    token = lax.broadcasted_iota(jnp.int32, (rows_count, 2 * moved_span), 0) % token_count
    lane = lax.broadcasted_iota(jnp.int32, (rows_count, 2 * moved_span), 1)
    seen = jnp.zeros((rows_count, 2 * moved_span), jnp.float32)
    odd = lax.rem(lax.axis_index("req"), 2)
    for block, side in enumerate((odd, 1 - odd)):
        position = lane - block * moved_span
        for n in range(request_count):
            bound = jnp.where(table_ref[n, 0] == target_ref[side, 0], length_ref[n], 0)
            inside = (position >= 0) & (position < moved_span) & (position < bound)
            seen = seen + jnp.where((token // draft_count == n) & inside, 1.0, 0.0)
    bias_ref[...] = jnp.where(seen > 0, 0.0, neg_big)


def local_attention(table, lengths, targets, queries, fresh_kv, pool_pages):
    token_count = queries.shape[0]
    moved = targets.shape[1]
    part = jax.ShapeDtypeStruct((KV_HEADS, HEADS // KV_HEADS * token_count, HEAD_DIM), jnp.float32)
    bias = jax.ShapeDtypeStruct((part.shape[1], 2 * moved * pool_pages.shape[1]), jnp.float32)
    return pl.pallas_call(
        local_attention_kernel,
        out_shape=(part, part, part, part, bias),
        in_specs=[pl.BlockSpec(memory_space=pltpu.SMEM)] * 3 + [pl.BlockSpec(memory_space=pltpu.VMEM)] * 3,
        out_specs=(pl.BlockSpec(memory_space=pltpu.VMEM),) * 5,
        compiler_params=pltpu.CompilerParams(vmem_limit_bytes=6 * 1024 * 1024),
        cost_estimate=pl.CostEstimate(flops=40 * 1024 * 1024, bytes_accessed=2 * 1024 * 1024, transcendentals=160 * 1024),
        name="local_attention",
    )(table, lengths, targets, queries, fresh_kv, pool_pages)


def arrived_attention_kernel(
    resid_ref, gain_ref, far_ref, near_ref, max_ref, sum_ref, out_ref, query_ref, bias_ref, residual_ref, normed_ref
):
    token_count, model_width = residual_ref.shape
    share = HEADS // KV_HEADS
    key_width = KV_HEADS * HEAD_DIM
    heads = range(KV_HEADS)

    def arrived(first):
        at = pl.ds(first, HEAD_DIM)
        return jnp.concatenate([far_ref[:, at], near_ref[:, at]], axis=0)

    scores = [
        lax.dot_general(
            query_ref[j].astype(jnp.bfloat16), arrived(j * HEAD_DIM), (((1,), (1,)), ((), ())),
            preferred_element_type=jnp.float32,
        )
        for j in heads
    ]
    hidden = bias_ref[...] < 0
    scores = [jnp.where(hidden, neg_big, part * HEAD_DIM ** (-0.5)) for part in scores]
    highest = [jnp.maximum(max_ref[j], jnp.max(scores[j], axis=1, keepdims=True)) for j in heads]
    weights = [jnp.exp(scores[j] - highest[j][:, :1]) for j in heads]
    scale = [jnp.exp(max_ref[j] - highest[j]) for j in heads]
    total = [sum_ref[j] * scale[j] + jnp.sum(weights[j], axis=1, keepdims=True) for j in heads]
    summed = [
        out_ref[j] * scale[j] + weighted_values(weights[j], arrived(key_width + j * HEAD_DIM)) for j in heads
    ]
    blocks = []
    for j in heads:
        attention = summed[j] / total[j]
        for h in range(share):
            first = (j * share + h) * HEAD_DIM
            resid = resid_ref[:, first : first + HEAD_DIM].astype(jnp.float32)
            blocks.append(resid + attention[h * token_count : (h + 1) * token_count])
    squares = blocks[0] * blocks[0]
    for block in blocks[1:]:
        squares = squares + block * block
    inv_rms = lax.rsqrt(jnp.sum(squares, axis=1, keepdims=True) / model_width + norm_eps)
    residual = jnp.concatenate(blocks, axis=1)
    residual_ref[...] = residual
    normed_ref[...] = (residual * inv_rms * gain_ref[...].astype(jnp.float32)[None, :]).astype(normed_ref.dtype)


def arrived_attention(resid_in, gain, far, near, parts):
    shape = resid_in.shape
    return pl.pallas_call(
        arrived_attention_kernel,
        out_shape=(jax.ShapeDtypeStruct(shape, jnp.float32), jax.ShapeDtypeStruct(shape, jnp.bfloat16)),
        in_specs=[pl.BlockSpec(memory_space=pltpu.VMEM)] * 9,
        out_specs=(pl.BlockSpec(memory_space=pltpu.VMEM),) * 2,
        compiler_params=pltpu.CompilerParams(vmem_limit_bytes=4 * 1024 * 1024),
        cost_estimate=pl.CostEstimate(flops=1024 * 1024 * 1024, bytes_accessed=2 * 1024 * 1024, transcendentals=60 * 1024),
        name="arrived_attention",
    )(resid_in, gain, far, near, *parts)


def pack_kernel(columns_ref, *refs):
    out_refs = refs[-EXP_DEV:]
    rows = jnp.concatenate([ref[...].astype(jnp.float32) for ref in refs[:-EXP_DEV]], axis=0)
    slots = jnp.dot(columns_ref[...], rows.astype(jnp.bfloat16), preferred_element_type=jnp.float32)
    for k, out_ref in enumerate(out_refs):
        out_ref[...] = slots[k * CAP : (k + 1) * CAP].astype(out_ref.dtype)


def pack(columns, parts):
    slots = jax.ShapeDtypeStruct((CAP, parts[0].shape[1]), parts[0].dtype)
    return pl.pallas_call(
        pack_kernel,
        out_shape=(slots,) * EXP_DEV,
        in_specs=[pl.BlockSpec(memory_space=pltpu.VMEM)] * (1 + len(parts)),
        out_specs=(pl.BlockSpec(memory_space=pltpu.VMEM),) * EXP_DEV,
        compiler_params=pltpu.CompilerParams(vmem_limit_bytes=8 * 1024 * 1024),
        cost_estimate=pl.CostEstimate(
            flops=8 * 1024 * 1024 * 1024, bytes_accessed=2 * 1024 * 1024, transcendentals=0
        ),
        name="pack",
    )(columns.reshape(EXP_DEV * CAP, -1), *parts)


def expert_kernel(rows_ref, inner_ref, outer_ref, *out_refs):
    rows = rows_ref[...]
    tile = min(2 * HEAD_DIM, inner_ref.shape[1])
    parts = []
    for c in range(0, inner_ref.shape[1], tile):
        hidden = jnp.dot(rows, inner_ref[:, c : c + tile], preferred_element_type=jnp.float32)
        parts.append((hidden / (1.0 + jnp.exp(-hidden))).astype(rows.dtype))
    activated = jnp.concatenate(parts, axis=1)
    tile = 2 * HEAD_DIM
    for c in range(0, outer_ref.shape[1], tile):
        out = jnp.dot(activated, outer_ref[:, c : c + tile], preferred_element_type=jnp.float32)
        for k, out_ref in enumerate(out_refs):
            out_ref[:, c : c + tile] = out[k * CAP : (k + 1) * CAP].astype(out_ref.dtype)


def expert(rows, inner, outer):
    width = outer.shape[1]
    others = rows.shape[0] // CAP - EXP_DEV
    out_shape = (jax.ShapeDtypeStruct((CAP, width), jnp.float32),) * EXP_DEV
    out_shape += (jax.ShapeDtypeStruct((CAP, width), rows.dtype),) * others
    return pl.pallas_call(
        expert_kernel,
        out_shape=out_shape,
        in_specs=[pl.BlockSpec(memory_space=pltpu.VMEM)] * 3,
        out_specs=(pl.BlockSpec(memory_space=pltpu.VMEM),) * len(out_shape),
        compiler_params=pltpu.CompilerParams(vmem_limit_bytes=32 * 1024 * 1024),
        cost_estimate=pl.CostEstimate(
            flops=2 * rows.shape[0] * (inner.size + outer.size),
            bytes_accessed=(inner.size + outer.size) * inner.dtype.itemsize,
            transcendentals=rows.shape[0] * inner.shape[1],
        ),
        name="expert",
    )(rows, inner, outer)


def combine_kernel(gate_ref, residual_ref, *refs):
    block_refs, out_refs = refs[:EXP_DEV], refs[EXP_DEV:]
    rows = jnp.concatenate([ref[...].astype(jnp.float32) for ref in block_refs], axis=0).astype(jnp.bfloat16)
    gates = jnp.concatenate([gate_ref[k] for k in RETURN_ORDER], axis=0)
    high = gates.astype(jnp.bfloat16)
    low = (gates - high.astype(jnp.float32)).astype(jnp.bfloat16)
    mix = lax.dot_general(
        jnp.concatenate([high.astype(jnp.float32), low.astype(jnp.float32)], axis=1).astype(jnp.bfloat16), rows,
        (((0,), (0,)), ((), ())), preferred_element_type=jnp.float32,
    )
    half = gates.shape[1]
    mix = mix[:half] + mix[half:]
    count = out_refs[0].shape[0]
    out_refs[0][...] = residual_ref[...] + mix[:count]
    for k, out_ref in enumerate(out_refs[1:]):
        out_ref[...] = mix[(k + 1) * count : (k + 2) * count].astype(out_ref.dtype)


def combine(gate_columns, residual, blocks, partners):
    sent = jax.ShapeDtypeStruct(residual.shape, jnp.bfloat16)
    return pl.pallas_call(
        combine_kernel,
        out_shape=(jax.ShapeDtypeStruct(residual.shape, jnp.float32),) + (sent,) * partners,
        in_specs=[pl.BlockSpec(memory_space=pltpu.VMEM)] * (2 + len(blocks)),
        out_specs=(pl.BlockSpec(memory_space=pltpu.VMEM),) * (1 + partners),
        compiler_params=pltpu.CompilerParams(vmem_limit_bytes=12 * 1024 * 1024),
        cost_estimate=pl.CostEstimate(
            flops=4 * gate_columns.size * residual.shape[1], bytes_accessed=4 * 1024 * 1024, transcendentals=0
        ),
        name="combine",
    )(gate_columns, residual, *[blocks[k] for k in RETURN_ORDER])


def body(
    resid_in,
    queries,
    fresh_kv,
    kv_pool,
    block_table,
    lengths,
    mig_source,
    mig_target,
    expert_ids,
    gate_values,
    norm_gain,
    w_in,
    w_out,
):
    token_count = resid_in.shape[0]
    model_width = resid_in.shape[1]
    exp_count = lax.axis_size("exp")
    group_size = lax.axis_size("req") // EXP_DEV
    plane_orders = PLANE_ORDERS
    member = lax.axis_index("req") % group_size
    group_steps = partner_steps(group_size)
    falling = list(range(exp_count - 1, 0, -1))
    exp_orders = (falling, falling[1::-1] + falling[2:])

    pool_pages = kv_pool[0, 0]
    targets = mig_target[0, 0]
    first = opening()
    far, near = (send_pages(pool_pages, mig_source[0, 0], first, far) for far in (True, False))
    moved_shape = (far.shape[0] * far.shape[1], far.shape[2])
    far = swap_ring(far.reshape(moved_shape), 1)
    near = swap_ring(near.reshape(moved_shape), 0)

    parts = local_attention(block_table, lengths, targets, queries, fresh_kv, pool_pages)
    residual, normed = arrived_attention(resid_in, norm_gain, far, near, parts)
    normed, expert_ids, gate_values = lax.optimization_barrier((normed, expert_ids, gate_values))

    exp_order = partner_of(lax.axis_index("exp"), exp_orders, member)
    plane_order = partner_of(lax.axis_index("req") // group_size, plane_orders, member)
    ids = expert_ids.reshape(exp_count, token_count, -1)[exp_order].reshape(expert_ids.shape)
    gates = gate_values.reshape(exp_count, token_count, -1)[exp_order].reshape(gate_values.shape)
    local_ids = lax.axis_index("exp") * EXP_DEV + plane_order
    matches = ids[None, :, :] == local_ids[:, None, None]
    is_named = jnp.any(matches, axis=2)
    gate_local = jnp.sum(jnp.where(matches, gates[None, :, :], 0.0), axis=2)
    slot_index = jnp.cumsum(is_named.astype(jnp.int32), axis=1) - 1
    placement = is_named[:, None, :] & (slot_index[:, None, :] == jnp.arange(CAP)[None, :, None])
    columns = placement.astype(jnp.bfloat16)
    gate_columns = jnp.where(placement, gate_local[:, None, :], 0.0)

    packed = pack(columns, [normed] + [swap_exp(normed, k, exp_orders, group_size) for k in range(exp_count - 1)])
    pieces = [packed[0]] + [
        swap_plane(packed[k + 1], k, plane_orders, group_size) for k in range(EXP_DEV - 1)
    ]
    inbound = jnp.concatenate(
        pieces + [swap_group(piece, step, group_size) for step in group_steps for piece in pieces], axis=0
    )

    slots = expert(inbound, w_in[0, 0], w_out[0, 0])
    summed = []
    for j in range(EXP_DEV):
        total = slots[j]
        for k, step in enumerate(group_steps):
            total = total + swap_group(slots[(k + 1) * EXP_DEV + j], step, group_size).astype(jnp.float32)
        summed.append(total.astype(jnp.bfloat16))

    returned = [summed[0]] + [
        swap_plane(summed[k + 1], k, plane_orders, group_size) for k in range(EXP_DEV - 1)
    ]
    result, *blocks = combine(gate_columns, residual, returned, exp_count - 1)
    for k in [0] + list(range(exp_count - 2, 0, -1)):
        result = result + swap_exp(blocks[k], k, exp_orders, group_size).astype(jnp.float32)
    return result.astype(jnp.bfloat16)


def solution(mesh):
    placed = (
        P(("req", "exp"), None),
        P(("req", "exp"), None),
        P(("req", "exp"), None),
        P("req", "exp", None, None, None),
        P(("req", "exp"), None),
        P(("req", "exp")),
        P("req", "exp", None, None),
        P("req", "exp", None, None),
        P("req", None),
        P("req", None),
        P(),
        P("exp", "req", None, None),
        P("exp", "req", None, None),
    )
    return jax.shard_map(
        body, mesh=mesh, in_specs=placed, out_specs=P(("req", "exp"), None), check_vma=False
    )
```

```python
import jax
import jax.numpy as jnp
from jax import lax
from jax.experimental import pallas as pl
from jax.experimental.pallas import tpu as pltpu
from jax.sharding import PartitionSpec as P

HEADS = 28
KV_HEADS = 4
HEAD_DIM = 128
EXP_DEV = 4
CAP = 24
PLANE_ORDERS = ((2, 3, 1), (1, 3, 2))
RETURN_ORDER = (0, 3, 2, 1)


neg_big = -1e30
norm_eps = 1e-06


def partner_steps(count):
    if count & (count - 1):
        raise ValueError("axis size")
    return [[i ^ k for i in range(count)] for k in range(1, count)]


def partner_of(index, orders, member):
    return index ^ jnp.array([[0] + list(order) for order in orders], dtype=jnp.int32)[member % len(orders)]


def swap_ring(block, offset):
    count = lax.axis_size("req")
    if count % 2:
        raise ValueError("axis size")
    pairs = []
    for i in range(offset, count, 2):
        pairs += [(i, (i + 1) % count), ((i + 1) % count, i)]
    return lax.ppermute(block, "req", pairs)


def swap_plane(block, k, orders, group_size):
    pairs = [
        (q * group_size + g, (q ^ orders[g % len(orders)][k]) * group_size + g)
        for q in range(EXP_DEV)
        for g in range(group_size)
    ]
    return lax.ppermute(block, "req", pairs)


def swap_group(block, step, group_size):
    pairs = [(q * group_size + g, q * group_size + p) for q in range(EXP_DEV) for g, p in enumerate(step)]
    return lax.ppermute(block, "req", pairs)


def swap_exp(block, k, orders, group_size):
    count = lax.axis_size("exp")
    pairs = [
        (r * count + e, r * count + (e ^ orders[r % group_size % len(orders)][k]))
        for r in range(lax.axis_size("req"))
        for e in range(count)
    ]
    return lax.ppermute(block, ("req", "exp"), pairs)


def opening_kernel(out_ref):
    out_ref[...] = jnp.zeros_like(out_ref)


def opening():
    return pl.pallas_call(
        opening_kernel,
        out_shape=jax.ShapeDtypeStruct((8, HEAD_DIM), jnp.float32),
        out_specs=pl.BlockSpec(memory_space=pltpu.VMEM),
        compiler_params=pltpu.CompilerParams(vmem_limit_bytes=1024 * 1024),
        cost_estimate=pl.CostEstimate(flops=4 * 1024 * 1024 * 1024, bytes_accessed=4096, transcendentals=0),
        name="opening",
    )()


def send_pages_kernel(source_ref, pool_ref, after_ref, far_ref, near_ref):
    odd = lax.rem(lax.axis_index("req"), 2)
    for side, out_ref in ((1 - odd, far_ref), (odd, near_ref)):
        for i in range(out_ref.shape[0]):
            out_ref[i] = pool_ref[source_ref[side, i]]


def send_pages(pool_pages, sources, after):
    pages = jax.ShapeDtypeStruct((sources.shape[1],) + pool_pages.shape[1:], pool_pages.dtype)
    return pl.pallas_call(
        send_pages_kernel,
        out_shape=(pages, pages),
        in_specs=[pl.BlockSpec(memory_space=pltpu.SMEM)] + [pl.BlockSpec(memory_space=pltpu.VMEM)] * 2,
        out_specs=(pl.BlockSpec(memory_space=pltpu.VMEM),) * 2,
        compiler_params=pltpu.CompilerParams(vmem_limit_bytes=4 * 1024 * 1024),
        cost_estimate=pl.CostEstimate(
            flops=4 * 1024 * 1024 * 1024, bytes_accessed=pool_pages.size * pool_pages.dtype.itemsize, transcendentals=0
        ),
        name="send_pages",
    )(sources, pool_pages, after)


def weighted_values(weights, values):
    high = weights.astype(jnp.bfloat16)
    low = (weights - high.astype(jnp.float32)).astype(jnp.bfloat16)
    both = jnp.dot(
        jnp.concatenate([high, low], axis=0), values, preferred_element_type=jnp.float32
    )
    return both[: weights.shape[0]] + both[weights.shape[0] :]


def local_attention_kernel(
    table_ref, length_ref, target_ref, queries_ref, fresh_ref, pool_ref, max_ref, sum_ref, out_ref, query_ref, bias_ref
):
    request_count, table_width = table_ref.shape
    token_count, kv_width = fresh_ref.shape
    moved = target_ref.shape[1]
    page_tokens = pool_ref.shape[1]
    span = table_width * page_tokens
    draft_count = token_count // request_count
    share = HEADS // KV_HEADS
    rows_count = share * token_count
    tail = HEAD_DIM
    query = queries_ref[...].astype(jnp.float32)
    fresh = jnp.concatenate(
        [
            fresh_ref[...].astype(jnp.float32),
            jnp.zeros((tail - token_count, kv_width), jnp.float32),
        ],
        axis=0,
    ).astype(fresh_ref.dtype)
    pages = [table_ref[n, i] for n in range(request_count) for i in range(table_width)]

    def cache(first):
        rows = [pool_ref[page, :, first : first + HEAD_DIM] for page in pages]
        return jnp.concatenate(rows + [fresh[:, first : first + HEAD_DIM]], axis=0)

    token = lax.broadcasted_iota(jnp.int32, (rows_count, span), 0) % token_count
    lane = lax.broadcasted_iota(jnp.int32, (rows_count, span), 1)
    live = []
    for n in range(request_count):
        arrives = (table_ref[n, 0] == target_ref[0, 0]) | (table_ref[n, 0] == target_ref[1, 0])
        first = jnp.where(arrives, moved * page_tokens, 0)
        live.append((token // draft_count == n) & (lane >= first) & (lane < length_ref[n]))
    tail_token = lax.broadcasted_iota(jnp.int32, (rows_count, tail), 0) % token_count
    tail_lane = lax.broadcasted_iota(jnp.int32, (rows_count, tail), 1)
    live.append((tail_token // draft_count == tail_lane // draft_count) & (tail_lane <= tail_token))
    live = jnp.concatenate([jnp.where(mask, 0.0, neg_big) for mask in live], axis=1)
    key_width = KV_HEADS * HEAD_DIM
    for j in range(KV_HEADS):
        heads = range(j * share, (j + 1) * share)
        rows = jnp.concatenate([query[:, h * HEAD_DIM : (h + 1) * HEAD_DIM] for h in heads], axis=0)
        query_ref[j] = rows
        scores = lax.dot_general(
            rows.astype(jnp.bfloat16), cache(j * HEAD_DIM), (((1,), (1,)), ((), ())),
            preferred_element_type=jnp.float32,
        )
        scores = jnp.where(live < 0, neg_big, scores * HEAD_DIM ** (-0.5))
        highest = jnp.max(scores, axis=1, keepdims=True)
        weights = jnp.exp(scores - highest)
        max_ref[j] = jnp.broadcast_to(highest, max_ref.shape[1:])
        sum_ref[j] = jnp.broadcast_to(jnp.sum(weights, axis=1, keepdims=True), sum_ref.shape[1:])
        out_ref[j] = weighted_values(weights, cache(key_width + j * HEAD_DIM))

    moved_span = moved * page_tokens
    token = lax.broadcasted_iota(jnp.int32, (rows_count, 2 * moved_span), 0) % token_count
    lane = lax.broadcasted_iota(jnp.int32, (rows_count, 2 * moved_span), 1)
    seen = jnp.zeros((rows_count, 2 * moved_span), jnp.float32)
    odd = lax.rem(lax.axis_index("req"), 2)
    for block, side in enumerate((odd, 1 - odd)):
        position = lane - block * moved_span
        for n in range(request_count):
            bound = jnp.where(table_ref[n, 0] == target_ref[side, 0], length_ref[n], 0)
            inside = (position >= 0) & (position < moved_span) & (position < bound)
            seen = seen + jnp.where((token // draft_count == n) & inside, 1.0, 0.0)
    bias_ref[...] = jnp.where(seen > 0, 0.0, neg_big)


def local_attention(table, lengths, targets, queries, fresh_kv, pool_pages):
    token_count = queries.shape[0]
    moved = targets.shape[1]
    part = jax.ShapeDtypeStruct((KV_HEADS, HEADS // KV_HEADS * token_count, HEAD_DIM), jnp.float32)
    bias = jax.ShapeDtypeStruct((part.shape[1], 2 * moved * pool_pages.shape[1]), jnp.float32)
    return pl.pallas_call(
        local_attention_kernel,
        out_shape=(part, part, part, part, bias),
        in_specs=[pl.BlockSpec(memory_space=pltpu.SMEM)] * 3 + [pl.BlockSpec(memory_space=pltpu.VMEM)] * 3,
        out_specs=(pl.BlockSpec(memory_space=pltpu.VMEM),) * 5,
        compiler_params=pltpu.CompilerParams(vmem_limit_bytes=6 * 1024 * 1024),
        cost_estimate=pl.CostEstimate(flops=40 * 1024 * 1024, bytes_accessed=2 * 1024 * 1024, transcendentals=160 * 1024),
        name="local_attention",
    )(table, lengths, targets, queries, fresh_kv, pool_pages)


def arrived_attention_kernel(
    resid_ref, gain_ref, far_ref, near_ref, max_ref, sum_ref, out_ref, query_ref, bias_ref, residual_ref, normed_ref
):
    token_count, model_width = residual_ref.shape
    share = HEADS // KV_HEADS
    key_width = KV_HEADS * HEAD_DIM
    heads = range(KV_HEADS)

    def arrived(first):
        at = pl.ds(first, HEAD_DIM)
        return jnp.concatenate([far_ref[:, at], near_ref[:, at]], axis=0)

    scores = [
        lax.dot_general(
            query_ref[j].astype(jnp.bfloat16), arrived(j * HEAD_DIM), (((1,), (1,)), ((), ())),
            preferred_element_type=jnp.float32,
        )
        for j in heads
    ]
    hidden = bias_ref[...] < 0
    scores = [jnp.where(hidden, neg_big, part * HEAD_DIM ** (-0.5)) for part in scores]
    highest = [jnp.maximum(max_ref[j], jnp.max(scores[j], axis=1, keepdims=True)) for j in heads]
    weights = [jnp.exp(scores[j] - highest[j][:, :1]) for j in heads]
    scale = [jnp.exp(max_ref[j] - highest[j]) for j in heads]
    total = [sum_ref[j] * scale[j] + jnp.sum(weights[j], axis=1, keepdims=True) for j in heads]
    summed = [
        out_ref[j] * scale[j] + weighted_values(weights[j], arrived(key_width + j * HEAD_DIM)) for j in heads
    ]
    blocks = []
    for j in heads:
        attention = summed[j] / total[j]
        for h in range(share):
            first = (j * share + h) * HEAD_DIM
            resid = resid_ref[:, first : first + HEAD_DIM].astype(jnp.float32)
            blocks.append(resid + attention[h * token_count : (h + 1) * token_count])
    squares = blocks[0] * blocks[0]
    for block in blocks[1:]:
        squares = squares + block * block
    inv_rms = lax.rsqrt(jnp.sum(squares, axis=1, keepdims=True) / model_width + norm_eps)
    residual = jnp.concatenate(blocks, axis=1)
    residual_ref[...] = residual
    normed_ref[...] = (residual * inv_rms * gain_ref[...].astype(jnp.float32)[None, :]).astype(normed_ref.dtype)


def arrived_attention(resid_in, gain, far, near, parts):
    shape = resid_in.shape
    return pl.pallas_call(
        arrived_attention_kernel,
        out_shape=(jax.ShapeDtypeStruct(shape, jnp.float32), jax.ShapeDtypeStruct(shape, jnp.bfloat16)),
        in_specs=[pl.BlockSpec(memory_space=pltpu.VMEM)] * 9,
        out_specs=(pl.BlockSpec(memory_space=pltpu.VMEM),) * 2,
        compiler_params=pltpu.CompilerParams(vmem_limit_bytes=4 * 1024 * 1024),
        cost_estimate=pl.CostEstimate(flops=1024 * 1024 * 1024, bytes_accessed=2 * 1024 * 1024, transcendentals=60 * 1024),
        name="arrived_attention",
    )(resid_in, gain, far, near, *parts)


def pack_kernel(columns_ref, *refs):
    out_refs = refs[-EXP_DEV:]
    rows = jnp.concatenate([ref[...].astype(jnp.float32) for ref in refs[:-EXP_DEV]], axis=0)
    slots = jnp.dot(columns_ref[...], rows.astype(jnp.bfloat16), preferred_element_type=jnp.float32)
    for k, out_ref in enumerate(out_refs):
        out_ref[...] = slots[k * CAP : (k + 1) * CAP].astype(out_ref.dtype)


def pack(columns, parts):
    slots = jax.ShapeDtypeStruct((CAP, parts[0].shape[1]), parts[0].dtype)
    return pl.pallas_call(
        pack_kernel,
        out_shape=(slots,) * EXP_DEV,
        in_specs=[pl.BlockSpec(memory_space=pltpu.VMEM)] * (1 + len(parts)),
        out_specs=(pl.BlockSpec(memory_space=pltpu.VMEM),) * EXP_DEV,
        compiler_params=pltpu.CompilerParams(vmem_limit_bytes=8 * 1024 * 1024),
        cost_estimate=pl.CostEstimate(
            flops=8 * 1024 * 1024 * 1024, bytes_accessed=2 * 1024 * 1024, transcendentals=0
        ),
        name="pack",
    )(columns.reshape(EXP_DEV * CAP, -1), *parts)


def expert_kernel(rows_ref, inner_ref, outer_ref, *out_refs):
    rows = rows_ref[...]
    tile = min(4 * HEAD_DIM, inner_ref.shape[1])
    parts = []
    for c in range(0, inner_ref.shape[1], tile):
        hidden = jnp.dot(rows, inner_ref[:, c : c + tile], preferred_element_type=jnp.float32)
        parts.append((hidden / (1.0 + jnp.exp(-hidden))).astype(rows.dtype))
    activated = jnp.concatenate(parts, axis=1)
    tile = 2 * HEAD_DIM
    for c in range(0, outer_ref.shape[1], tile):
        out = jnp.dot(activated, outer_ref[:, c : c + tile], preferred_element_type=jnp.float32)
        for k, out_ref in enumerate(out_refs):
            out_ref[:, c : c + tile] = out[k * CAP : (k + 1) * CAP].astype(out_ref.dtype)


def expert(rows, inner, outer):
    width = outer.shape[1]
    others = rows.shape[0] // CAP - EXP_DEV
    out_shape = (jax.ShapeDtypeStruct((CAP, width), jnp.float32),) * EXP_DEV
    out_shape += (jax.ShapeDtypeStruct((CAP, width), rows.dtype),) * others
    return pl.pallas_call(
        expert_kernel,
        out_shape=out_shape,
        in_specs=[pl.BlockSpec(memory_space=pltpu.VMEM)] * 3,
        out_specs=(pl.BlockSpec(memory_space=pltpu.VMEM),) * len(out_shape),
        compiler_params=pltpu.CompilerParams(vmem_limit_bytes=32 * 1024 * 1024),
        cost_estimate=pl.CostEstimate(
            flops=2 * rows.shape[0] * (inner.size + outer.size),
            bytes_accessed=(inner.size + outer.size) * inner.dtype.itemsize,
            transcendentals=rows.shape[0] * inner.shape[1],
        ),
        name="expert",
    )(rows, inner, outer)


def combine_kernel(gate_ref, residual_ref, *refs):
    block_refs, out_refs = refs[:EXP_DEV], refs[EXP_DEV:]
    rows = jnp.concatenate([ref[...].astype(jnp.float32) for ref in block_refs], axis=0).astype(jnp.bfloat16)
    gates = jnp.concatenate([gate_ref[k] for k in RETURN_ORDER], axis=0)
    high = gates.astype(jnp.bfloat16)
    low = (gates - high.astype(jnp.float32)).astype(jnp.bfloat16)
    mix = lax.dot_general(
        jnp.concatenate([high.astype(jnp.float32), low.astype(jnp.float32)], axis=1).astype(jnp.bfloat16), rows,
        (((0,), (0,)), ((), ())), preferred_element_type=jnp.float32,
    )
    half = gates.shape[1]
    mix = mix[:half] + mix[half:]
    count = out_refs[0].shape[0]
    out_refs[0][...] = residual_ref[...] + mix[:count]
    for k, out_ref in enumerate(out_refs[1:]):
        out_ref[...] = mix[(k + 1) * count : (k + 2) * count].astype(out_ref.dtype)


def combine(gate_columns, residual, blocks, partners):
    sent = jax.ShapeDtypeStruct(residual.shape, jnp.bfloat16)
    return pl.pallas_call(
        combine_kernel,
        out_shape=(jax.ShapeDtypeStruct(residual.shape, jnp.float32),) + (sent,) * partners,
        in_specs=[pl.BlockSpec(memory_space=pltpu.VMEM)] * (2 + len(blocks)),
        out_specs=(pl.BlockSpec(memory_space=pltpu.VMEM),) * (1 + partners),
        compiler_params=pltpu.CompilerParams(vmem_limit_bytes=12 * 1024 * 1024),
        cost_estimate=pl.CostEstimate(
            flops=4 * gate_columns.size * residual.shape[1], bytes_accessed=4 * 1024 * 1024, transcendentals=0
        ),
        name="combine",
    )(gate_columns, residual, *[blocks[k] for k in RETURN_ORDER])


def body(
    resid_in,
    queries,
    fresh_kv,
    kv_pool,
    block_table,
    lengths,
    mig_source,
    mig_target,
    expert_ids,
    gate_values,
    norm_gain,
    w_in,
    w_out,
):
    token_count = resid_in.shape[0]
    model_width = resid_in.shape[1]
    exp_count = lax.axis_size("exp")
    group_size = lax.axis_size("req") // EXP_DEV
    plane_orders = PLANE_ORDERS
    member = lax.axis_index("req") % group_size
    group_steps = partner_steps(group_size)
    falling = list(range(exp_count - 1, 0, -1))
    exp_orders = (falling, falling[1::-1] + falling[2:])

    pool_pages = kv_pool[0, 0]
    targets = mig_target[0, 0]
    far, near = send_pages(pool_pages, mig_source[0, 0], opening())
    moved_shape = (far.shape[0] * far.shape[1], far.shape[2])
    far = swap_ring(far.reshape(moved_shape), 1)
    near = swap_ring(near.reshape(moved_shape), 0)

    parts = local_attention(block_table, lengths, targets, queries, fresh_kv, pool_pages)
    residual, normed = arrived_attention(resid_in, norm_gain, far, near, parts)
    normed, expert_ids, gate_values = lax.optimization_barrier((normed, expert_ids, gate_values))

    exp_order = partner_of(lax.axis_index("exp"), exp_orders, member)
    plane_order = partner_of(lax.axis_index("req") // group_size, plane_orders, member)
    ids = expert_ids.reshape(exp_count, token_count, -1)[exp_order].reshape(expert_ids.shape)
    gates = gate_values.reshape(exp_count, token_count, -1)[exp_order].reshape(gate_values.shape)
    local_ids = lax.axis_index("exp") * EXP_DEV + plane_order
    matches = ids[None, :, :] == local_ids[:, None, None]
    is_named = jnp.any(matches, axis=2)
    gate_local = jnp.sum(jnp.where(matches, gates[None, :, :], 0.0), axis=2)
    slot_index = jnp.cumsum(is_named.astype(jnp.int32), axis=1) - 1
    placement = is_named[:, None, :] & (slot_index[:, None, :] == jnp.arange(CAP)[None, :, None])
    columns = placement.astype(jnp.bfloat16)
    gate_columns = jnp.where(placement, gate_local[:, None, :], 0.0)

    packed = pack(columns, [normed] + [swap_exp(normed, k, exp_orders, group_size) for k in range(exp_count - 1)])
    pieces = [packed[0]] + [
        swap_plane(packed[k + 1], k, plane_orders, group_size) for k in range(EXP_DEV - 1)
    ]
    inbound = jnp.concatenate(
        pieces + [swap_group(piece, step, group_size) for step in group_steps for piece in pieces], axis=0
    )

    slots = expert(inbound, w_in[0, 0], w_out[0, 0])
    summed = []
    for j in range(EXP_DEV):
        total = slots[j]
        for k, step in enumerate(group_steps):
            total = total + swap_group(slots[(k + 1) * EXP_DEV + j], step, group_size).astype(jnp.float32)
        summed.append(total.astype(jnp.bfloat16))

    returned = [summed[0]] + [
        swap_plane(summed[k + 1], k, plane_orders, group_size) for k in range(EXP_DEV - 1)
    ]
    result, *blocks = combine(gate_columns, residual, returned, exp_count - 1)
    for k in [0] + list(range(exp_count - 2, 0, -1)):
        result = result + swap_exp(blocks[k], k, exp_orders, group_size).astype(jnp.float32)
    return result.astype(jnp.bfloat16)


def solution(mesh):
    placed = (
        P(("req", "exp"), None),
        P(("req", "exp"), None),
        P(("req", "exp"), None),
        P("req", "exp", None, None, None),
        P(("req", "exp"), None),
        P(("req", "exp")),
        P("req", "exp", None, None),
        P("req", "exp", None, None),
        P("req", None),
        P("req", None),
        P(),
        P("exp", "req", None, None),
        P("exp", "req", None, None),
    )
    return jax.shard_map(
        body, mesh=mesh, in_specs=placed, out_specs=P(("req", "exp"), None), check_vma=False
    )
```
